128 devices in a mesh: tensor: 4 (over x_lo, core), fsdp: 32 (over y, x_hi, z).
Axes of the slice: x: 4 (x_hi: 2, x_lo: 2; x = x_hi * 2 + x_lo), y: 4, z: 4, core: 2. Of those that a mesh axis runs over, the one named last changes fastest.
Arguments:
- grad: bfloat16 [1, 8192, 15360], P(None, 'fsdp', 'tensor'), may hold values from -18 to 18
- left_roots: bfloat16 [1, 8192, 15360], P(None, 'fsdp', 'tensor'), may hold values from -1 to 2
- right_roots: bfloat16 [1, 8192, 15360], P(None, 'fsdp', 'tensor'), may hold values from -1 to 2
Outputs:
- left_stats: float32 [1, 8192, 15360], P(None, 'fsdp', 'tensor')
- right_stats: float32 [1, 8192, 15360], P(None, 'fsdp', 'tensor')
- update: bfloat16 [1, 8192, 15360], P(None, 'fsdp', 'tensor')
The draws below stay inside these ranges and needn't reach their ends.
All inputs are finite; a program needn't handle non-finite values.
Results may differ from the reference program's by a relative error of at most 0.0055.
Values may be sent and summed in bfloat16 or wider, within the bound.
A program may use at most 192 MiB of HBM per device.

```python
import math
import jax
import jax.numpy as jnp
from jax import lax

D = 8192
FF = 15360
BLK = 1024
LAYERS = 1


def diagonal_mask():
    row_position = jnp.arange(D) % BLK
    col_position = jnp.arange(FF) % BLK
    return (row_position[:, None] == col_position[None, :]).astype(jnp.float32)


def draw_grad(key, part):
    key = jax.random.fold_in(key, 5)
    full_shape = (LAYERS, D, FF)
    row_frac = jnp.arange(D).astype(jnp.float32) / max(D - 1, 1)
    col_frac = jnp.arange(FF).astype(jnp.float32) / max(FF - 1, 1)
    spread = 0.5 * math.log(3.0)
    noise_part = jnp.clip(jax.random.normal(key, full_shape, jnp.float32), -6.0, 6.0)
    row_scale = jnp.exp(spread * (2.0 * row_frac - 1.0))
    col_scale = jnp.exp(spread * (2.0 * col_frac - 1.0))
    return (noise_part * row_scale[:, None] * col_scale[None, :]).astype(jnp.bfloat16)


def draw_left_roots(key, part):
    key = jax.random.fold_in(key, 11)
    noise_key = jax.random.fold_in(key, 0)
    full_shape = (LAYERS, D, FF)
    noise_part = jnp.clip(jax.random.normal(noise_key, full_shape, jnp.float32), -4.0, 4.0)
    diag_part = jnp.ones(full_shape, jnp.float32)
    return (diagonal_mask() * diag_part + noise_part * (0.6 / math.sqrt(BLK))).astype(jnp.bfloat16)


def draw_right_roots(key, part):
    key = jax.random.fold_in(key, 23)
    noise_key = jax.random.fold_in(key, 0)
    full_shape = (LAYERS, D, FF)
    noise_part = jnp.clip(jax.random.normal(noise_key, full_shape, jnp.float32), -4.0, 4.0)
    diag_part = jnp.ones(full_shape, jnp.float32)
    return (diagonal_mask() * diag_part + noise_part * (0.6 / math.sqrt(BLK))).astype(jnp.bfloat16)


def setup_inputs(seed: int = 0) -> dict:
    key_of = jax.random.split(jax.random.key(seed), 4)
    return {
        "grad": draw_grad(jax.random.fold_in(key_of[3], 71), 0),
        "left_roots": draw_left_roots(jax.random.fold_in(key_of[3], 71), 0),
        "right_roots": draw_right_roots(jax.random.fold_in(key_of[3], 71), 0),
    }


def reference(grad, left_roots, right_roots):
    row_blocks = D // BLK
    col_blocks = FF // BLK
    inverse_width = 1.0 / BLK
    highest = lax.Precision.HIGHEST
    left_list = []
    right_list = []
    update_list = []
    for layer_index in range(LAYERS):
        blocks = grad[layer_index].astype(jnp.float32).reshape(row_blocks, BLK, col_blocks, BLK)
        left_stat = jnp.einsum('iajc,ibjc->iajb', blocks, blocks, precision=highest) * inverse_width
        right_stat = jnp.einsum('irjd,irje->idje', blocks, blocks, precision=highest) * inverse_width
        left_block_roots = left_roots[layer_index].astype(jnp.float32).reshape(row_blocks, BLK, col_blocks, BLK)
        right_block_roots = right_roots[layer_index].astype(jnp.float32).reshape(row_blocks, BLK, col_blocks, BLK)
        applied = jnp.einsum('iajb,ibjd->iajd', left_block_roots, blocks, precision=highest).astype(jnp.bfloat16)
        applied = lax.optimization_barrier(applied).astype(jnp.float32)
        preconditioned = jnp.einsum('iajd,idje->iaje', applied, right_block_roots, precision=highest)
        square_sum = jnp.sum(preconditioned * preconditioned)
        scale = 1.0 / jnp.sqrt(square_sum / (D * FF) + 1e-06)
        update = (preconditioned * scale).astype(jnp.bfloat16)
        left_list.append(left_stat.reshape(D, FF))
        right_list.append(right_stat.reshape(D, FF))
        update_list.append(update.reshape(D, FF))
    return (jnp.stack(left_list), jnp.stack(right_list), jnp.stack(update_list))
```

```python
import functools

import jax
import jax.numpy as jnp
from jax import lax
from jax.experimental import pallas as pl
from jax.experimental.pallas import tpu as pltpu
from jax.sharding import PartitionSpec as P

D = 8192
FF = 15360
BLK = 1024
Q = 256
RING = 4
COLS = 3840
MESH = pl.DeviceIdType.MESH


def matmul(a, b):
    return lax.dot_general(a, b, (((1,), (0,)), ((), ())), preferred_element_type=jnp.float32)


def matmul_nt(a, b):
    return lax.dot_general(a, b, (((1,), (1,)), ((), ())), preferred_element_type=jnp.float32)


def kernel(
    grad, left_roots, right_roots, left_out, right_out, update_out, scale_out,
    own, blocks, roots, other_left, flipped, applied, away, home, edge, sums, landed,
    load_sem, piece_sem, halo_sem, send_sem, recv_sem, sum_sem, store_sem, edge_sem,
):
    inputs = (grad, left_roots, right_roots)
    outputs = (left_out, right_out, update_out)
    t = lax.axis_index("tensor")
    f = lax.axis_index("fsdp")
    z = lax.rem(f, RING)
    g = lax.div(f, RING)
    inner = jnp.logical_or(t == 1, t == 2)
    first_half = t < 2

    def along(step):
        return lax.rem(z + step + RING, RING)

    def z_device(step):
        return {"fsdp": g * RING + along(step)}

    def t_device(step):
        return {"tensor": lax.rem(t + step, 4)}

    def g_device(bit):
        other = g + bit - 2 * bit * lax.rem(lax.div(g, bit), 2)
        return {"fsdp": other * RING + z}

    def rows(quarter):
        return pl.ds(pl.multiple_of(quarter * Q, Q), Q)

    def cols(start, size):
        return pl.ds(pl.multiple_of(start, Q), size)

    loads = []
    for kind in (0, 1, 2):
        for slot in range(3):
            loads.append(pltpu.make_async_copy(
                inputs[kind].at[0, :, cols(Q * t + BLK * slot, BLK)], own.at[kind, slot], load_sem.at[kind, slot]
            ))
    for copy in loads:
        copy.start()

    barrier = pltpu.get_barrier_semaphore()
    partners = [z_device(i) for i in (1, 2, 3)] + [t_device(i) for i in (1, 2, 3)] + [g_device(b) for b in (1, 2, 4)]
    for device in partners:
        pl.semaphore_signal(barrier, inc=1, device_id=device, device_id_type=MESH)
    pl.semaphore_wait(barrier, len(partners))

    def outer_piece(kind):
        return pltpu.make_async_copy(
            inputs[kind].at[0, :, cols(jnp.where(first_half, 3072, 0), 768)],
            own.at[kind, 3, :, cols(jnp.where(first_half, 0, 256), 768)],
            piece_sem.at[kind],
        )

    def inner_piece(kind):
        return pltpu.make_async_copy(
            inputs[kind].at[0, :, cols(jnp.where(first_half, 3328, 0), 512)],
            own.at[kind, 3, :, cols(jnp.where(first_half, 0, 512), 512)],
            piece_sem.at[kind],
        )

    def half_over(kind):
        return pltpu.make_async_remote_copy(
            src_ref=inputs[kind].at[0, :, cols(jnp.where(first_half, 3328, 0), 512)],
            dst_ref=own.at[kind, 3, :, cols(jnp.where(first_half, 0, 512), 512)],
            send_sem=halo_sem.at[0, kind], recv_sem=halo_sem.at[1, kind],
            device_id={"tensor": 3 - t}, device_id_type=MESH,
        )

    def quarter_over(kind):
        return pltpu.make_async_remote_copy(
            src_ref=inputs[kind].at[0, :, cols(jnp.where(first_half, 0, 3584), 256)],
            dst_ref=own.at[kind, 3, :, cols(jnp.where(first_half, 768, 0), 256)],
            send_sem=halo_sem.at[2, kind], recv_sem=halo_sem.at[3, kind],
            device_id={"tensor": jnp.where(first_half, 0, 3)}, device_id_type=MESH,
        )

    def quarter_arrives(kind):
        return pltpu.make_async_remote_copy(
            src_ref=own.at[kind, 3, :, cols(jnp.where(first_half, 768, 0), 256)],
            dst_ref=own.at[kind, 3, :, cols(jnp.where(first_half, 768, 0), 256)],
            send_sem=halo_sem.at[2, kind], recv_sem=halo_sem.at[3, kind],
            device_id={"tensor": jnp.where(first_half, 1, 2)}, device_id_type=MESH,
        )

    @pl.when(inner)
    def _():
        for kind in (0, 1, 2):
            half_over(kind).start()
            quarter_over(kind).start()
            inner_piece(kind).start()

    @pl.when(jnp.logical_not(inner))
    def _():
        for kind in (0, 1, 2):
            outer_piece(kind).start()

    def loaded(kind):
        for slot in range(3):
            loads[3 * kind + slot].wait()

        @pl.when(inner)
        def _():
            inner_piece(kind).wait()
            half_over(kind).wait()
            quarter_over(kind).wait_send()

        @pl.when(jnp.logical_not(inner))
        def _():
            outer_piece(kind).wait()
            quarter_arrives(kind).wait_recv()

    def send(number, way, source, target):
        return pltpu.make_async_remote_copy(
            src_ref=source, dst_ref=target,
            send_sem=send_sem.at[number, way], recv_sem=recv_sem.at[number, way],
            device_id=z_device(1 if way == 0 else 3), device_id_type=MESH,
        )

    own_slot = (along(0), along(-1))
    feed_slot = (along(1), along(2))
    behind = (along(-1), along(1))

    def send_own(number, way, kind, full):
        return send(number, way, own.at[kind, own_slot[way]], full.at[1 - way, rows(z)])

    def send_feed(number, way, kind, full):
        return send(number, way, own.at[kind, feed_slot[way]], full.at[way, rows(z)])

    def send_on(number, way, full):
        return send(number, way, full.at[way, rows(behind[way])], full.at[1 - way, rows(behind[way])])

    def send_left(number, way):
        return send(number, way, own.at[1, feed_slot[way]], other_left.at[way])

    def send_back(number, way, kind):
        return send(number, way, away.at[kind, 1 - way], home.at[kind, along(-1) if way == 0 else along(0)])

    both = (0, 1)
    b_feed = [send_feed(0, way, 0, blocks) for way in both]
    b_own = [send_own(1, way, 0, blocks) for way in both]
    b_on = [send_on(2, way, blocks) for way in both]
    l_feed = [send_left(3, way) for way in both]
    r_feed = [send_feed(4, way, 2, roots) for way in both]
    r_own = [send_own(5, way, 2, roots) for way in both]
    r_on = [send_on(6, way, roots) for way in both]
    back = [[send_back(7 + kind, way, kind) for way in both] for kind in (0, 1, 2)]

    def start(copies):
        for copy in copies:
            copy.start()

    def arrive(copies):
        for copy in copies:
            copy.wait_recv()

    loaded(0)
    start(b_feed)
    start(b_own)
    loaded(1)
    start(l_feed)
    loaded(2)
    start(r_feed)
    for role in both:
        blocks[role, rows(z), :] = own[0, own_slot[role]]
        roots[role, rows(z), :] = own[2, own_slot[role]]
    arrive(b_feed)
    start(b_on)
    start(r_own)
    arrive(b_own)
    arrive(b_on)
    arrive(l_feed)

    def compute_stats(role, mine):
        quarter = z if mine else behind[role]
        slot = own_slot[role]
        flipped[...] = blocks[role, :, cols(quarter * Q, Q)].T

        def tile(n, carry):
            window = cols(n * Q, Q)
            left = matmul_nt(blocks[role, rows(quarter), :], blocks[role, rows(n), :])
            left = (left * (1.0 / BLK)).astype(jnp.bfloat16)
            right = matmul(flipped[...], blocks[role, :, window])
            right = (right * (1.0 / BLK)).astype(jnp.bfloat16)
            left_rows = own[1, slot] if mine else other_left[role]
            applied[role, 1 if mine else 0, :, window] = matmul(left_rows, blocks[role, :, window]).astype(jnp.bfloat16)
            if mine:
                home[0, slot, :, window] = left
                home[1, slot, :, window] = right
            else:
                away[0, role, :, window] = left
                away[1, role, :, window] = right
            return carry

        lax.fori_loop(0, 4, tile, 0)

    compute_stats(0, False)
    compute_stats(1, False)
    arrive(r_feed)
    start(r_on)
    start(back[0])
    compute_stats(0, True)
    compute_stats(1, True)
    arrive(r_own)
    arrive(r_on)
    start(back[1])

    sums[0] = jnp.zeros((8, 128), jnp.float32)

    def compute_update(role, mine):
        slot = own_slot[role]
        split = jnp.logical_and(slot == 3, inner)

        def tile(n, carry):
            window = cols(n * Q, Q)
            value = matmul(applied[role, 1 if mine else 0], roots[role, :, window])
            if mine:
                home[2, slot, :, window] = value.astype(jnp.bfloat16)
            else:
                away[2, role, :, window] = value.astype(jnp.bfloat16)
            squares = jnp.sum((value * value).reshape(Q // 8, 8, Q), axis=0)
            squares = squares[:, :128] + squares[:, 128:]
            counted = jnp.logical_or(jnp.logical_not(split), (n < 2) == first_half)
            sums[0] += jnp.where(counted, squares, 0.0)
            return carry

        lax.fori_loop(0, 4, tile, 0)

    compute_update(0, False)
    compute_update(1, False)
    start(back[2])
    compute_update(0, True)
    compute_update(1, True)

    def share(stage, number, device):
        return pltpu.make_async_remote_copy(
            src_ref=sums.at[stage], dst_ref=landed.at[number],
            send_sem=sum_sem.at[0, number], recv_sem=sum_sem.at[1, number],
            device_id=device, device_id_type=MESH,
        )

    stages = [
        [(i - 1, z_device(i)) for i in (1, 2, 3)],
        [(i + 2, t_device(i)) for i in (1, 2, 3)],
        [(6, g_device(1))],
        [(7, g_device(2))],
        [(8, g_device(4))],
    ]
    for stage, group in enumerate(stages):
        copies = [share(stage, number, device) for number, device in group]
        start(copies)
        total = sums[stage]
        for copy in copies:
            copy.wait()
        for number, _ in group:
            total = total + landed[number]
        sums[stage + 1] = total
    square_sum = jnp.sum(sums[len(stages)])
    scale_out[...] = 1.0 / jnp.sqrt(jnp.full((8, 128), square_sum) * (1.0 / (D * FF)) + 1e-06)

    def store(kind, slot):
        return pltpu.make_async_copy(
            home.at[kind, slot], outputs[kind].at[0, :, cols(Q * t + BLK * slot, BLK)], store_sem.at[kind, slot]
        )

    def outer_store(kind):
        return pltpu.make_async_copy(
            home.at[kind, 3, :, cols(jnp.where(first_half, 0, 256), 768)],
            outputs[kind].at[0, :, cols(jnp.where(first_half, 3072, 0), 768)],
            store_sem.at[kind, 3],
        )

    def inner_store(kind):
        return pltpu.make_async_copy(
            home.at[kind, 3, :, cols(jnp.where(first_half, 0, 512), 512)],
            outputs[kind].at[0, :, cols(jnp.where(first_half, 3328, 0), 512)],
            store_sem.at[kind, 3],
        )

    def edge_store(kind):
        return pltpu.make_async_copy(
            edge.at[kind], outputs[kind].at[0, :, cols(jnp.where(first_half, 0, 3584), 256)], store_sem.at[kind, 4]
        )

    def edge_over(kind):
        return pltpu.make_async_remote_copy(
            src_ref=home.at[kind, 3, :, cols(jnp.where(first_half, 768, 0), 256)], dst_ref=edge.at[kind],
            send_sem=edge_sem.at[0, kind], recv_sem=edge_sem.at[1, kind],
            device_id={"tensor": jnp.where(first_half, 1, 2)}, device_id_type=MESH,
        )

    def edge_arrives(kind):
        return pltpu.make_async_remote_copy(
            src_ref=edge.at[kind], dst_ref=edge.at[kind],
            send_sem=edge_sem.at[0, kind], recv_sem=edge_sem.at[1, kind],
            device_id={"tensor": jnp.where(first_half, 0, 3)}, device_id_type=MESH,
        )

    for kind in (0, 1, 2):
        arrive(back[kind])

        @pl.when(jnp.logical_not(inner))
        def _():
            edge_over(kind).start()
            outer_store(kind).start()

        @pl.when(inner)
        def _():
            inner_store(kind).start()

        for slot in range(3):
            store(kind, slot).start()

    for kind in (0, 1, 2):
        @pl.when(inner)
        def _():
            edge_arrives(kind).wait_recv()
            edge_store(kind).start()

    for kind in (0, 1, 2):
        for slot in range(3):
            store(kind, slot).wait()

        @pl.when(inner)
        def _():
            inner_store(kind).wait()
            edge_store(kind).wait()

        @pl.when(jnp.logical_not(inner))
        def _():
            outer_store(kind).wait()
            edge_over(kind).wait_send()

    for copies in [b_feed, b_own, b_on, l_feed, r_feed, r_own, r_on] + back:
        for copy in copies:
            copy.wait_send()


def shards(grad, left_roots, right_roots):
    half = jnp.bfloat16
    out = jax.ShapeDtypeStruct((1, Q, COLS), half)
    hbm = pl.BlockSpec(memory_space=pl.ANY)
    dma = pltpu.SemaphoreType.DMA
    left, right, update, scale = pl.pallas_call(
        kernel,
        out_shape=[out, out, out, jax.ShapeDtypeStruct((8, 128), jnp.float32)],
        in_specs=[hbm] * 3,
        out_specs=[hbm] * 3 + [pl.BlockSpec(memory_space=pltpu.VMEM)],
        scratch_shapes=[
            pltpu.VMEM((3, 4, Q, BLK), half),
            pltpu.VMEM((2, BLK, BLK), half),
            pltpu.VMEM((2, BLK, BLK), half),
            pltpu.VMEM((2, Q, BLK), half),
            pltpu.VMEM((Q, BLK), half),
            pltpu.VMEM((2, 2, Q, BLK), half),
            pltpu.VMEM((3, 2, Q, BLK), half),
            pltpu.VMEM((3, 4, Q, BLK), half),
            pltpu.VMEM((3, Q, Q), half),
            pltpu.VMEM((6, 8, 128), jnp.float32),
            pltpu.VMEM((9, 8, 128), jnp.float32),
            dma((3, 3)), dma((3,)), dma((4, 3)), dma((10, 2)), dma((10, 2)), dma((2, 9)), dma((3, 5)), dma((2, 3)),
        ],
        compiler_params=pltpu.CompilerParams(
            collective_id=0, has_side_effects=True, vmem_limit_bytes=48 * 1024 * 1024
        ),
        cost_estimate=pl.CostEstimate(flops=8_600_000_000, bytes_accessed=12_000_000, transcendentals=0),
    )(grad, left_roots, right_roots)
    scale = scale[0, 0]
    update = (update.astype(jnp.float32) * scale).astype(half)
    return left.astype(jnp.float32), right.astype(jnp.float32), update


def solution(mesh):
    spec = P(None, "fsdp", "tensor")
    return jax.shard_map(shards, mesh=mesh, in_specs=(spec,) * 3, out_specs=(spec,) * 3, check_vma=False)
```

```python
import functools

import jax
import jax.numpy as jnp
from jax import lax
from jax.experimental import pallas as pl
from jax.experimental.pallas import tpu as pltpu
from jax.sharding import PartitionSpec as P

D = 8192
FF = 15360
BLK = 1024
Q = 256
RING = 4
COLS = 3840
MESH = pl.DeviceIdType.MESH


def matmul(a, b):
    return lax.dot_general(a, b, (((1,), (0,)), ((), ())), preferred_element_type=jnp.float32)


def matmul_nt(a, b):
    return lax.dot_general(a, b, (((1,), (1,)), ((), ())), preferred_element_type=jnp.float32)


def kernel(
    grad, left_roots, right_roots, left_out, right_out, update_out, scale_out,
    own, blocks, roots, other_left, flipped, applied, away, home, edge, sums, landed,
    load_sem, piece_sem, halo_sem, send_sem, recv_sem, sum_sem, store_sem, edge_sem,
):
    inputs = (grad, left_roots, right_roots)
    outputs = (left_out, right_out, update_out)
    t = lax.axis_index("tensor")
    f = lax.axis_index("fsdp")
    z = lax.rem(f, RING)
    g = lax.div(f, RING)
    inner = jnp.logical_or(t == 1, t == 2)
    first_half = t < 2

    def along(step):
        return lax.rem(z + step + RING, RING)

    def z_device(step):
        return {"fsdp": g * RING + along(step)}

    def t_device(step):
        return {"tensor": lax.rem(t + step, 4)}

    def g_device(bit):
        other = g + bit - 2 * bit * lax.rem(lax.div(g, bit), 2)
        return {"fsdp": other * RING + z}

    def rows(quarter):
        return pl.ds(pl.multiple_of(quarter * Q, Q), Q)

    def cols(start, size):
        return pl.ds(pl.multiple_of(start, Q), size)

    loads = []
    for kind in (0, 1, 2):
        for slot in range(3):
            loads.append(pltpu.make_async_copy(
                inputs[kind].at[0, :, cols(Q * t + BLK * slot, BLK)], own.at[kind, slot], load_sem.at[kind, slot]
            ))
    for copy in loads:
        copy.start()

    barrier = pltpu.get_barrier_semaphore()
    partners = [z_device(i) for i in (1, 2, 3)] + [t_device(i) for i in (1, 2, 3)] + [g_device(b) for b in (1, 2, 4)]
    for device in partners:
        pl.semaphore_signal(barrier, inc=1, device_id=device, device_id_type=MESH)
    pl.semaphore_wait(barrier, len(partners))

    def outer_piece(kind):
        return pltpu.make_async_copy(
            inputs[kind].at[0, :, cols(jnp.where(first_half, 3072, 0), 768)],
            own.at[kind, 3, :, cols(jnp.where(first_half, 0, 256), 768)],
            piece_sem.at[kind],
        )

    def inner_piece(kind):
        return pltpu.make_async_copy(
            inputs[kind].at[0, :, cols(jnp.where(first_half, 3328, 0), 512)],
            own.at[kind, 3, :, cols(jnp.where(first_half, 0, 512), 512)],
            piece_sem.at[kind],
        )

    def half_over(kind):
        return pltpu.make_async_remote_copy(
            src_ref=inputs[kind].at[0, :, cols(jnp.where(first_half, 3328, 0), 512)],
            dst_ref=own.at[kind, 3, :, cols(jnp.where(first_half, 0, 512), 512)],
            send_sem=halo_sem.at[0, kind], recv_sem=halo_sem.at[1, kind],
            device_id={"tensor": 3 - t}, device_id_type=MESH,
        )

    def quarter_over(kind):
        return pltpu.make_async_remote_copy(
            src_ref=inputs[kind].at[0, :, cols(jnp.where(first_half, 0, 3584), 256)],
            dst_ref=own.at[kind, 3, :, cols(jnp.where(first_half, 768, 0), 256)],
            send_sem=halo_sem.at[2, kind], recv_sem=halo_sem.at[3, kind],
            device_id={"tensor": jnp.where(first_half, 0, 3)}, device_id_type=MESH,
        )

    def quarter_arrives(kind):
        return pltpu.make_async_remote_copy(
            src_ref=own.at[kind, 3, :, cols(jnp.where(first_half, 768, 0), 256)],
            dst_ref=own.at[kind, 3, :, cols(jnp.where(first_half, 768, 0), 256)],
            send_sem=halo_sem.at[2, kind], recv_sem=halo_sem.at[3, kind],
            device_id={"tensor": jnp.where(first_half, 1, 2)}, device_id_type=MESH,
        )

    @pl.when(inner)
    def _():
        for kind in (0, 1, 2):
            half_over(kind).start()
            quarter_over(kind).start()
            inner_piece(kind).start()

    @pl.when(jnp.logical_not(inner))
    def _():
        for kind in (0, 1, 2):
            outer_piece(kind).start()

    def loaded_whole(kind):
        for slot in range(3):
            loads[3 * kind + slot].wait()

    def loaded_pieces(kind):
        @pl.when(inner)
        def _():
            inner_piece(kind).wait()
            half_over(kind).wait()
            quarter_over(kind).wait_send()

        @pl.when(jnp.logical_not(inner))
        def _():
            outer_piece(kind).wait()
            quarter_arrives(kind).wait_recv()

    def send(number, way, source, target):
        return pltpu.make_async_remote_copy(
            src_ref=source, dst_ref=target,
            send_sem=send_sem.at[number, way], recv_sem=recv_sem.at[number, way],
            device_id=z_device(1 if way == 0 else 3), device_id_type=MESH,
        )

    own_slot = (along(0), along(-1))
    feed_slot = (along(1), along(2))
    behind = (along(-1), along(1))

    def send_own(number, way, kind, full):
        return send(number, way, own.at[kind, own_slot[way]], full.at[1 - way, rows(z)])

    def send_feed(number, way, kind, full):
        return send(number, way, own.at[kind, feed_slot[way]], full.at[way, rows(z)])

    def send_on(number, way, full):
        return send(number, way, full.at[way, rows(behind[way])], full.at[1 - way, rows(behind[way])])

    def send_left(number, way):
        return send(number, way, own.at[1, feed_slot[way]], other_left.at[way])

    def send_back(number, way, kind):
        return send(number, way, away.at[kind, 1 - way], home.at[kind, along(-1) if way == 0 else along(0)])

    both = (0, 1)
    b_feed = [send_feed(0, way, 0, blocks) for way in both]
    b_own = [send_own(1, way, 0, blocks) for way in both]
    b_on = [send_on(2, way, blocks) for way in both]
    l_feed = [send_left(3, way) for way in both]
    r_feed = [send_feed(4, way, 2, roots) for way in both]
    r_own = [send_own(5, way, 2, roots) for way in both]
    r_on = [send_on(6, way, roots) for way in both]
    def send_back_tile(step, way):
        quarter = lax.rem(behind[1 - way] + step, RING)
        window = cols(quarter * Q, Q)
        return send(
            8 + step if step > 1 else 7, way, away.at[0, 1 - way, :, window],
            home.at[0, along(-1) if way == 0 else along(0), :, window],
        )

    back = [
        [send_back_tile(step, way) for step in (1, 2, 3) for way in both],
        [send_back(8, way, 1) for way in both],
        [send_back(9, way, 2) for way in both],
    ]

    def start(copies):
        for copy in copies:
            copy.start()

    def arrive(copies):
        for copy in copies:
            copy.wait_recv()

    def start_where(whole):
        for way in both:
            for copy, slot in ((b_feed[way], feed_slot[way]), (b_own[way], own_slot[way])):
                pl.when((slot < 3) == whole)(copy.start)

    loaded_whole(0)
    start_where(True)
    loaded_pieces(0)
    start_where(False)
    loaded_whole(1)
    loaded_pieces(1)
    start(l_feed)
    loaded_whole(2)
    loaded_pieces(2)
    start(r_feed)
    for role in both:
        blocks[role, rows(z), :] = own[0, own_slot[role]]
        roots[role, rows(z), :] = own[2, own_slot[role]]
    arrive(b_feed)
    start(b_on)
    start(r_own)
    arrive(b_own)
    arrive(b_on)
    arrive(l_feed)

    def compute_stats(role, mine):
        quarter = z if mine else behind[role]
        slot = own_slot[role]
        flipped[...] = blocks[role, :, cols(quarter * Q, Q)].T

        def tile(n, carry):
            window = cols(n * Q, Q)
            left = matmul_nt(blocks[role, rows(quarter), :], blocks[role, rows(n), :])
            left = (left * (1.0 / BLK)).astype(jnp.bfloat16)
            right = matmul(flipped[...], blocks[role, :, window])
            right = (right * (1.0 / BLK)).astype(jnp.bfloat16)
            left_rows = own[1, slot] if mine else other_left[role]
            applied[role, 1 if mine else 0, :, window] = matmul(left_rows, blocks[role, :, window]).astype(jnp.bfloat16)
            if mine:
                home[0, slot, :, window] = left
                home[1, slot, :, window] = right
            else:
                away[0, role, :, window] = left
                away[1, role, :, window] = right
            return carry

        lax.fori_loop(0, 4, tile, 0)

    for way in both:
        feed = own[0, feed_slot[way]]
        tile = (matmul_nt(feed, feed) * (1.0 / BLK)).astype(jnp.bfloat16)
        home[0, feed_slot[way], :, cols(z * Q, Q)] = tile
    compute_stats(0, False)
    compute_stats(1, False)
    arrive(r_feed)
    start(r_on)
    start(back[0])
    compute_stats(0, True)
    compute_stats(1, True)
    arrive(r_own)
    arrive(r_on)

    sums[0] = jnp.zeros((8, 128), jnp.float32)

    def compute_update(role, mine):
        slot = own_slot[role]
        split = jnp.logical_and(slot == 3, inner)

        def tile(n, carry):
            window = cols(n * Q, Q)
            value = matmul(applied[role, 1 if mine else 0], roots[role, :, window])
            if mine:
                home[2, slot, :, window] = value.astype(jnp.bfloat16)
            else:
                away[2, role, :, window] = value.astype(jnp.bfloat16)
            squares = jnp.sum((value * value).reshape(Q // 8, 8, Q), axis=0)
            squares = squares[:, :128] + squares[:, 128:]
            counted = jnp.logical_or(jnp.logical_not(split), (n < 2) == first_half)
            sums[0] += jnp.where(counted, squares, 0.0)
            return carry

        lax.fori_loop(0, 4, tile, 0)

    compute_update(0, False)
    compute_update(1, False)
    compute_update(0, True)
    compute_update(1, True)

    def share(stage, number, device):
        return pltpu.make_async_remote_copy(
            src_ref=sums.at[stage], dst_ref=landed.at[number],
            send_sem=sum_sem.at[0, number], recv_sem=sum_sem.at[1, number],
            device_id=device, device_id_type=MESH,
        )

    stages = [
        [(i - 1, z_device(i)) for i in (1, 2, 3)],
        [(i + 2, t_device(i)) for i in (1, 2, 3)],
        [(6, g_device(1))],
        [(7, g_device(2))],
        [(8, g_device(4))],
    ]
    for stage, group in enumerate(stages):
        copies = [share(stage, number, device) for number, device in group]
        start(copies)
        if stage == 0:
            start(back[1])
            start(back[2])
        total = sums[stage]
        for copy in copies:
            copy.wait()
        for number, _ in group:
            total = total + landed[number]
        sums[stage + 1] = total
    square_sum = jnp.sum(sums[len(stages)])
    scale_out[...] = 1.0 / jnp.sqrt(jnp.full((8, 128), square_sum) * (1.0 / (D * FF)) + 1e-06)

    def store(kind, slot):
        return pltpu.make_async_copy(
            home.at[kind, slot], outputs[kind].at[0, :, cols(Q * t + BLK * slot, BLK)], store_sem.at[kind, slot]
        )

    def outer_store(kind):
        return pltpu.make_async_copy(
            home.at[kind, 3, :, cols(jnp.where(first_half, 0, 256), 768)],
            outputs[kind].at[0, :, cols(jnp.where(first_half, 3072, 0), 768)],
            store_sem.at[kind, 3],
        )

    def inner_store(kind):
        return pltpu.make_async_copy(
            home.at[kind, 3, :, cols(jnp.where(first_half, 0, 512), 512)],
            outputs[kind].at[0, :, cols(jnp.where(first_half, 3328, 0), 512)],
            store_sem.at[kind, 3],
        )

    def edge_store(kind):
        return pltpu.make_async_copy(
            edge.at[kind], outputs[kind].at[0, :, cols(jnp.where(first_half, 0, 3584), 256)], store_sem.at[kind, 4]
        )

    def edge_over(kind):
        return pltpu.make_async_remote_copy(
            src_ref=home.at[kind, 3, :, cols(jnp.where(first_half, 768, 0), 256)], dst_ref=edge.at[kind],
            send_sem=edge_sem.at[0, kind], recv_sem=edge_sem.at[1, kind],
            device_id={"tensor": jnp.where(first_half, 1, 2)}, device_id_type=MESH,
        )

    def edge_arrives(kind):
        return pltpu.make_async_remote_copy(
            src_ref=edge.at[kind], dst_ref=edge.at[kind],
            send_sem=edge_sem.at[0, kind], recv_sem=edge_sem.at[1, kind],
            device_id={"tensor": jnp.where(first_half, 0, 3)}, device_id_type=MESH,
        )

    for kind in (0, 1, 2):
        arrive(back[kind])

        @pl.when(jnp.logical_not(inner))
        def _():
            edge_over(kind).start()
            outer_store(kind).start()

        @pl.when(inner)
        def _():
            inner_store(kind).start()

        for slot in range(3):
            store(kind, slot).start()

    for kind in (0, 1, 2):
        @pl.when(inner)
        def _():
            edge_arrives(kind).wait_recv()
            edge_store(kind).start()

    for kind in (0, 1, 2):
        for slot in range(3):
            store(kind, slot).wait()

        @pl.when(inner)
        def _():
            inner_store(kind).wait()
            edge_store(kind).wait()

        @pl.when(jnp.logical_not(inner))
        def _():
            outer_store(kind).wait()
            edge_over(kind).wait_send()

    for copies in [b_feed, b_own, b_on, l_feed, r_feed, r_own, r_on] + back:
        for copy in copies:
            copy.wait_send()


def shards(grad, left_roots, right_roots):
    half = jnp.bfloat16
    out = jax.ShapeDtypeStruct((1, Q, COLS), half)
    hbm = pl.BlockSpec(memory_space=pl.ANY)
    dma = pltpu.SemaphoreType.DMA
    left, right, update, scale = pl.pallas_call(
        kernel,
        out_shape=[out, out, out, jax.ShapeDtypeStruct((8, 128), jnp.float32)],
        in_specs=[hbm] * 3,
        out_specs=[hbm] * 3 + [pl.BlockSpec(memory_space=pltpu.VMEM)],
        scratch_shapes=[
            pltpu.VMEM((3, 4, Q, BLK), half),
            pltpu.VMEM((2, BLK, BLK), half),
            pltpu.VMEM((2, BLK, BLK), half),
            pltpu.VMEM((2, Q, BLK), half),
            pltpu.VMEM((Q, BLK), half),
            pltpu.VMEM((2, 2, Q, BLK), half),
            pltpu.VMEM((3, 2, Q, BLK), half),
            pltpu.VMEM((3, 4, Q, BLK), half),
            pltpu.VMEM((3, Q, Q), half),
            pltpu.VMEM((6, 8, 128), jnp.float32),
            pltpu.VMEM((9, 8, 128), jnp.float32),
            dma((3, 3)), dma((3,)), dma((4, 3)), dma((12, 2)), dma((12, 2)), dma((2, 9)), dma((3, 5)), dma((2, 3)),
        ],
        compiler_params=pltpu.CompilerParams(
            collective_id=0, has_side_effects=True, vmem_limit_bytes=48 * 1024 * 1024
        ),
        cost_estimate=pl.CostEstimate(flops=8_600_000_000, bytes_accessed=12_000_000, transcendentals=0),
    )(grad, left_roots, right_roots)
    scale = scale[0, 0]
    update = (update.astype(jnp.float32) * scale).astype(half)
    return left.astype(jnp.float32), right.astype(jnp.float32), update


def solution(mesh):
    spec = P(None, "fsdp", "tensor")
    return jax.shard_map(shards, mesh=mesh, in_specs=(spec,) * 3, out_specs=(spec,) * 3, check_vma=False)
```

```python
import functools

import jax
import jax.numpy as jnp
from jax import lax
from jax.experimental import pallas as pl
from jax.experimental.pallas import tpu as pltpu
from jax.sharding import PartitionSpec as P

D = 8192
FF = 15360
BLK = 1024
Q = 256
RING = 4
COLS = 3840
MESH = pl.DeviceIdType.MESH


def matmul(a, b):
    return lax.dot_general(a, b, (((1,), (0,)), ((), ())), preferred_element_type=jnp.float32)


def matmul_nt(a, b):
    return lax.dot_general(a, b, (((1,), (1,)), ((), ())), preferred_element_type=jnp.float32)


def kernel(
    grad, left_roots, right_roots, left_out, right_out, update_out, scale_out,
    own, blocks, roots, other_left, flipped, applied, away, home, edge, sums, landed,
    load_sem, piece_sem, halo_sem, send_sem, recv_sem, sum_sem, store_sem, edge_sem,
):
    inputs = (grad, left_roots, right_roots)
    outputs = (left_out, right_out, update_out)
    t = lax.axis_index("tensor")
    f = lax.axis_index("fsdp")
    z = lax.rem(f, RING)
    g = lax.div(f, RING)
    inner = jnp.logical_or(t == 1, t == 2)
    first_half = t < 2

    def along(step):
        return lax.rem(z + step + RING, RING)

    def z_device(step):
        return {"fsdp": g * RING + along(step)}

    def t_device(step):
        return {"tensor": lax.rem(t + step, 4)}

    def g_device(bit):
        other = g + bit - 2 * bit * lax.rem(lax.div(g, bit), 2)
        return {"fsdp": other * RING + z}

    def rows(quarter):
        return pl.ds(pl.multiple_of(quarter * Q, Q), Q)

    def cols(start, size):
        return pl.ds(pl.multiple_of(start, Q), size)

    loads = []
    for kind in (0, 1, 2):
        for slot in range(3):
            loads.append(pltpu.make_async_copy(
                inputs[kind].at[0, :, cols(Q * t + BLK * slot, BLK)], own.at[kind, slot], load_sem.at[kind, slot]
            ))
    for copy in loads:
        copy.start()

    barrier = pltpu.get_barrier_semaphore()
    partners = [z_device(i) for i in (1, 2, 3)] + [t_device(i) for i in (1, 2, 3)] + [g_device(b) for b in (1, 2, 4)]
    for device in partners:
        pl.semaphore_signal(barrier, inc=1, device_id=device, device_id_type=MESH)
    pl.semaphore_wait(barrier, len(partners))

    def outer_piece(kind):
        return pltpu.make_async_copy(
            inputs[kind].at[0, :, cols(jnp.where(first_half, 3072, 0), 768)],
            own.at[kind, 3, :, cols(jnp.where(first_half, 0, 256), 768)],
            piece_sem.at[kind],
        )

    def inner_piece(kind):
        return pltpu.make_async_copy(
            inputs[kind].at[0, :, cols(jnp.where(first_half, 3328, 0), 512)],
            own.at[kind, 3, :, cols(jnp.where(first_half, 0, 512), 512)],
            piece_sem.at[kind],
        )

    def half_over(kind):
        return pltpu.make_async_remote_copy(
            src_ref=inputs[kind].at[0, :, cols(jnp.where(first_half, 3328, 0), 512)],
            dst_ref=own.at[kind, 3, :, cols(jnp.where(first_half, 0, 512), 512)],
            send_sem=halo_sem.at[0, kind], recv_sem=halo_sem.at[1, kind],
            device_id={"tensor": 3 - t}, device_id_type=MESH,
        )

    def quarter_over(kind):
        return pltpu.make_async_remote_copy(
            src_ref=inputs[kind].at[0, :, cols(jnp.where(first_half, 0, 3584), 256)],
            dst_ref=own.at[kind, 3, :, cols(jnp.where(first_half, 768, 0), 256)],
            send_sem=halo_sem.at[2, kind], recv_sem=halo_sem.at[3, kind],
            device_id={"tensor": jnp.where(first_half, 0, 3)}, device_id_type=MESH,
        )

    def quarter_arrives(kind):
        return pltpu.make_async_remote_copy(
            src_ref=own.at[kind, 3, :, cols(jnp.where(first_half, 768, 0), 256)],
            dst_ref=own.at[kind, 3, :, cols(jnp.where(first_half, 768, 0), 256)],
            send_sem=halo_sem.at[2, kind], recv_sem=halo_sem.at[3, kind],
            device_id={"tensor": jnp.where(first_half, 1, 2)}, device_id_type=MESH,
        )

    @pl.when(inner)
    def _():
        for kind in (0, 1, 2):
            half_over(kind).start()
            quarter_over(kind).start()
            inner_piece(kind).start()

    @pl.when(jnp.logical_not(inner))
    def _():
        for kind in (0, 1, 2):
            outer_piece(kind).start()

    def loaded_whole(kind):
        for slot in range(3):
            loads[3 * kind + slot].wait()

    def loaded_pieces(kind):
        @pl.when(inner)
        def _():
            inner_piece(kind).wait()
            half_over(kind).wait()
            quarter_over(kind).wait_send()

        @pl.when(jnp.logical_not(inner))
        def _():
            outer_piece(kind).wait()
            quarter_arrives(kind).wait_recv()

    def send(number, way, source, target):
        return pltpu.make_async_remote_copy(
            src_ref=source, dst_ref=target,
            send_sem=send_sem.at[number, way], recv_sem=recv_sem.at[number, way],
            device_id=z_device(1 if way == 0 else 3), device_id_type=MESH,
        )

    own_slot = (along(0), along(-1))
    feed_slot = (along(1), along(2))
    behind = (along(-1), along(1))

    def send_own(number, way, kind, full):
        return send(number, way, own.at[kind, own_slot[way]], full.at[1 - way, rows(z)])

    def send_feed(number, way, kind, full):
        return send(number, way, own.at[kind, feed_slot[way]], full.at[way, rows(z)])

    def send_on(number, way, full):
        return send(number, way, full.at[way, rows(behind[way])], full.at[1 - way, rows(behind[way])])

    def send_left(number, way):
        return send(number, way, own.at[1, feed_slot[way]], other_left.at[way])

    def send_back(number, way, kind):
        return send(number, way, away.at[kind, 1 - way], home.at[kind, along(-1) if way == 0 else along(0)])

    both = (0, 1)
    b_feed = [send_feed(0, way, 0, blocks) for way in both]
    b_own = [send_own(1, way, 0, blocks) for way in both]
    b_on = [send_on(2, way, blocks) for way in both]
    l_feed = [send_left(3, way) for way in both]
    r_feed = [send_feed(4, way, 2, roots) for way in both]
    r_own = [send_own(5, way, 2, roots) for way in both]
    r_on = [send_on(6, way, roots) for way in both]
    def send_back_tile(step, way):
        quarter = lax.rem(behind[1 - way] + step, RING)
        window = cols(quarter * Q, Q)
        return send(
            8 + step if step > 1 else 7, way, away.at[0, 1 - way, :, window],
            home.at[0, along(-1) if way == 0 else along(0), :, window],
        )

    back = [
        [send_back_tile(step, way) for step in (1, 2, 3) for way in both],
        [send_back(8, way, 1) for way in both],
        [send_back(9, way, 2) for way in both],
    ]

    def start(copies):
        for copy in copies:
            copy.start()

    def arrive(copies):
        for copy in copies:
            copy.wait_recv()

    def start_where(whole):
        for way in both:
            for copy, slot in ((b_feed[way], feed_slot[way]), (b_own[way], own_slot[way])):
                pl.when((slot < 3) == whole)(copy.start)

    loaded_whole(0)
    start_where(True)
    loaded_pieces(0)
    start_where(False)
    loaded_whole(1)
    loaded_pieces(1)
    start(l_feed)
    loaded_whole(2)
    loaded_pieces(2)
    start(r_feed)
    for role in both:
        blocks[role, rows(z), :] = own[0, own_slot[role]]
        roots[role, rows(z), :] = own[2, own_slot[role]]
    arrive(b_feed)
    start(b_on)
    start(r_own)
    arrive(b_own)
    arrive(b_on)
    arrive(l_feed)

    def compute_stats(role, mine):
        quarter = z if mine else behind[role]
        slot = own_slot[role]
        flipped[...] = blocks[role, :, cols(quarter * Q, Q)].T

        def tile(n, carry):
            window = cols(n * Q, Q)
            left = matmul_nt(blocks[role, rows(quarter), :], blocks[role, rows(n), :])
            left = (left * (1.0 / BLK)).astype(jnp.bfloat16)
            right = matmul(flipped[...], blocks[role, :, window])
            right = (right * (1.0 / BLK)).astype(jnp.bfloat16)
            left_rows = own[1, slot] if mine else other_left[role]
            applied[role, 1 if mine else 0, :, window] = matmul(left_rows, blocks[role, :, window]).astype(jnp.bfloat16)
            if mine:
                home[0, slot, :, window] = left
                home[1, slot, :, window] = right
            else:
                away[0, role, :, window] = left
                away[1, role, :, window] = right
            return carry

        lax.fori_loop(0, 4, tile, 0)

    for way in both:
        feed = own[0, feed_slot[way]]
        tile = (matmul_nt(feed, feed) * (1.0 / BLK)).astype(jnp.bfloat16)
        home[0, feed_slot[way], :, cols(z * Q, Q)] = tile
    compute_stats(0, False)
    compute_stats(1, False)
    arrive(r_feed)
    start(r_on)
    start(back[0])
    compute_stats(0, True)
    compute_stats(1, True)
    arrive(r_own)
    arrive(r_on)

    sums[0] = jnp.zeros((8, 128), jnp.float32)

    def compute_update(role, mine):
        slot = own_slot[role]
        split = jnp.logical_and(slot == 3, inner)

        def tile(n, carry):
            window = cols(n * Q, Q)
            value = matmul(applied[role, 1 if mine else 0], roots[role, :, window])
            if mine:
                home[2, slot, :, window] = value.astype(jnp.bfloat16)
            else:
                away[2, role, :, window] = value.astype(jnp.bfloat16)
            squares = jnp.sum((value * value).reshape(Q // 8, 8, Q), axis=0)
            squares = squares[:, :128] + squares[:, 128:]
            counted = jnp.logical_or(jnp.logical_not(split), (n < 2) == first_half)
            sums[0] += jnp.where(counted, squares, 0.0)
            return carry

        lax.fori_loop(0, 4, tile, 0)

    compute_update(0, False)
    compute_update(1, False)
    compute_update(0, True)
    compute_update(1, True)

    def share(stage, number, device):
        return pltpu.make_async_remote_copy(
            src_ref=sums.at[stage], dst_ref=landed.at[number],
            send_sem=sum_sem.at[0, number], recv_sem=sum_sem.at[1, number],
            device_id=device, device_id_type=MESH,
        )

    stages = [
        [(i - 1, z_device(i)) for i in (1, 2, 3)],
        [(i + 2, t_device(i)) for i in (1, 2, 3)],
        [(6, g_device(1))],
        [(7, g_device(2))],
        [(8, g_device(4))],
    ]
    for stage, group in enumerate(stages):
        copies = [share(stage, number, device) for number, device in group]
        start(copies)
        if stage == 0:
            start(back[1])
            start(back[2])
        total = sums[stage]
        for copy in copies:
            copy.wait()
        for number, _ in group:
            total = total + landed[number]
        sums[stage + 1] = total
    square_sum = jnp.sum(sums[len(stages)])
    scale_out[...] = 1.0 / jnp.sqrt(jnp.full((8, 128), square_sum) * (1.0 / (D * FF)) + 1e-06)

    def store(kind, slot):
        return pltpu.make_async_copy(
            home.at[kind, slot], outputs[kind].at[0, :, cols(Q * t + BLK * slot, BLK)], store_sem.at[kind, slot]
        )

    def outer_store(kind):
        return pltpu.make_async_copy(
            home.at[kind, 3, :, cols(jnp.where(first_half, 0, 256), 768)],
            outputs[kind].at[0, :, cols(jnp.where(first_half, 3072, 0), 768)],
            store_sem.at[kind, 3],
        )

    def inner_store(kind):
        return pltpu.make_async_copy(
            home.at[kind, 3, :, cols(jnp.where(first_half, 0, 512), 512)],
            outputs[kind].at[0, :, cols(jnp.where(first_half, 3328, 0), 512)],
            store_sem.at[kind, 3],
        )

    def edge_store(kind):
        return pltpu.make_async_copy(
            edge.at[kind], outputs[kind].at[0, :, cols(jnp.where(first_half, 0, 3584), 256)], store_sem.at[kind, 4]
        )

    def edge_over(kind):
        return pltpu.make_async_remote_copy(
            src_ref=home.at[kind, 3, :, cols(jnp.where(first_half, 768, 0), 256)], dst_ref=edge.at[kind],
            send_sem=edge_sem.at[0, kind], recv_sem=edge_sem.at[1, kind],
            device_id={"tensor": jnp.where(first_half, 1, 2)}, device_id_type=MESH,
        )

    def edge_arrives(kind):
        return pltpu.make_async_remote_copy(
            src_ref=edge.at[kind], dst_ref=edge.at[kind],
            send_sem=edge_sem.at[0, kind], recv_sem=edge_sem.at[1, kind],
            device_id={"tensor": jnp.where(first_half, 0, 3)}, device_id_type=MESH,
        )

    for kind in (0, 1, 2):
        arrive(back[kind])

        @pl.when(jnp.logical_not(inner))
        def _():
            edge_over(kind).start()
            outer_store(kind).start()

        @pl.when(inner)
        def _():
            inner_store(kind).start()

        for slot in range(3):
            store(kind, slot).start()

    for kind in (0, 1, 2):
        @pl.when(inner)
        def _():
            edge_arrives(kind).wait_recv()
            edge_store(kind).start()

    for kind in (0, 1, 2):
        for slot in range(3):
            store(kind, slot).wait()

        @pl.when(inner)
        def _():
            inner_store(kind).wait()
            edge_store(kind).wait()

        @pl.when(jnp.logical_not(inner))
        def _():
            outer_store(kind).wait()
            edge_over(kind).wait_send()

    for copies in [b_feed, b_own, b_on, l_feed, r_feed, r_own, r_on] + back:
        for copy in copies:
            copy.wait_send()


def shards(grad, left_roots, right_roots):
    half = jnp.bfloat16
    out = jax.ShapeDtypeStruct((1, Q, COLS), half)
    hbm = pl.BlockSpec(memory_space=pl.ANY)
    dma = pltpu.SemaphoreType.DMA
    left, right, update, scale = pl.pallas_call(
        kernel,
        out_shape=[out, out, out, jax.ShapeDtypeStruct((8, 128), jnp.float32)],
        in_specs=[pl.BlockSpec(memory_space=pltpu.HBM)] * 3,
        out_specs=[hbm] * 3 + [pl.BlockSpec(memory_space=pltpu.VMEM)],
        scratch_shapes=[
            pltpu.VMEM((3, 4, Q, BLK), half),
            pltpu.VMEM((2, BLK, BLK), half),
            pltpu.VMEM((2, BLK, BLK), half),
            pltpu.VMEM((2, Q, BLK), half),
            pltpu.VMEM((Q, BLK), half),
            pltpu.VMEM((2, 2, Q, BLK), half),
            pltpu.VMEM((3, 2, Q, BLK), half),
            pltpu.VMEM((3, 4, Q, BLK), half),
            pltpu.VMEM((3, Q, Q), half),
            pltpu.VMEM((6, 8, 128), jnp.float32),
            pltpu.VMEM((9, 8, 128), jnp.float32),
            dma((3, 3)), dma((3,)), dma((4, 3)), dma((12, 2)), dma((12, 2)), dma((2, 9)), dma((3, 5)), dma((2, 3)),
        ],
        compiler_params=pltpu.CompilerParams(
            collective_id=0, has_side_effects=True, vmem_limit_bytes=30 * 1024 * 1024
        ),
        cost_estimate=pl.CostEstimate(flops=8_600_000_000, bytes_accessed=12_000_000, transcendentals=0),
    )(*[pltpu.with_memory_space_constraint(a, pltpu.HBM) for a in (grad, left_roots, right_roots)])
    return finish(left, right, update, scale)


def finish_kernel(left, right, update, scale, left_out, right_out, update_out, wide, narrow, sem):
    part = 64
    copies = []
    slot = 0
    for start in range(0, Q, part):
        rows = pl.ds(start, part)
        for source, target in ((left, left_out), (right, right_out)):
            wide[slot] = source[0, rows, :].astype(jnp.float32)
            copies.append(pltpu.make_async_copy(wide.at[slot], target.at[0, rows, :], sem.at[len(copies)]))
            copies[-1].start()
            slot += 1
        narrow[rows, :] = (update[0, rows, :].astype(jnp.float32) * scale[0:1, 0:1]).astype(jnp.bfloat16)
        copies.append(pltpu.make_async_copy(narrow.at[rows, :], update_out.at[0, rows, :], sem.at[len(copies)]))
        copies[-1].start()
    for copy in copies:
        copy.wait()


def finish(left, right, update, scale):
    shape = (1, Q, COLS)
    return tuple(pl.pallas_call(
        finish_kernel,
        out_shape=[jax.ShapeDtypeStruct(shape, d) for d in (jnp.float32, jnp.float32, jnp.bfloat16)],
        in_specs=[pl.BlockSpec(memory_space=pltpu.VMEM)] * 4,
        out_specs=[pl.BlockSpec(memory_space=pl.ANY)] * 3,
        scratch_shapes=[
            pltpu.VMEM((8, 64, COLS), jnp.float32), pltpu.VMEM((Q, COLS), jnp.bfloat16), pltpu.SemaphoreType.DMA((12,))
        ],
        compiler_params=pltpu.CompilerParams(vmem_limit_bytes=16 * 1024 * 1024),
    )(left, right, update, scale))


def solution(mesh):
    spec = P(None, "fsdp", "tensor")
    return jax.shard_map(shards, mesh=mesh, in_specs=(spec,) * 3, out_specs=(spec,) * 3, check_vma=False)
```

```python
import functools

import jax
import jax.numpy as jnp
from jax import lax
from jax.experimental import pallas as pl
from jax.experimental.pallas import tpu as pltpu
from jax.sharding import PartitionSpec as P

D = 8192
FF = 15360
BLK = 1024
Q = 256
RING = 4
COLS = 3840
MESH = pl.DeviceIdType.MESH


def matmul(a, b):
    return lax.dot_general(a, b, (((1,), (0,)), ((), ())), preferred_element_type=jnp.float32)


def matmul_nt(a, b):
    return lax.dot_general(a, b, (((1,), (1,)), ((), ())), preferred_element_type=jnp.float32)


def kernel(
    grad, left_roots, right_roots, left_out, right_out, update_out, scale_out,
    own, blocks, roots, other_left, flipped, applied, away, home, edge, transit, sums, landed,
    load_sem, piece_sem, halo_sem, send_sem, recv_sem, sum_sem, store_sem, edge_sem,
):
    inputs = (grad, left_roots, right_roots)
    outputs = (left_out, right_out, update_out)
    t = lax.axis_index("tensor")
    f = lax.axis_index("fsdp")
    z = lax.rem(f, RING)
    g = lax.div(f, RING)
    inner = jnp.logical_or(t == 1, t == 2)
    outer = jnp.logical_not(inner)
    first_half = t < 2

    def along(step):
        return lax.rem(z + step + RING, RING)

    def z_device(step):
        return {"fsdp": g * RING + along(step)}

    def t_device(step):
        return {"tensor": lax.rem(t + step, 4)}

    def g_device(bit):
        other = g + bit - 2 * bit * lax.rem(lax.div(g, bit), 2)
        return {"fsdp": other * RING + z}

    def rows(quarter):
        return pl.ds(pl.multiple_of(quarter * Q, Q), Q)

    def cols(start, size):
        return pl.ds(pl.multiple_of(start, Q), size)

    loads = []
    for kind in (0, 1, 2):
        for slot in range(3):
            loads.append(pltpu.make_async_copy(
                inputs[kind].at[0, :, cols(Q * t + BLK * slot, BLK)], own.at[kind, slot], load_sem.at[kind, slot]
            ))
    for copy in loads:
        copy.start()

    barrier = pltpu.get_barrier_semaphore()
    partners = [z_device(i) for i in (1, 2, 3)] + [t_device(i) for i in (1, 2, 3)] + [g_device(b) for b in (1, 2, 4)]
    for device in partners:
        pl.semaphore_signal(barrier, inc=1, device_id=device, device_id_type=MESH)
    pl.semaphore_wait(barrier, len(partners))

    def outer_piece(kind):
        return pltpu.make_async_copy(
            inputs[kind].at[0, :, cols(jnp.where(first_half, 3072, 0), 768)],
            own.at[kind, 3, :, cols(jnp.where(first_half, 0, 256), 768)],
            piece_sem.at[kind],
        )

    def inner_piece(kind):
        return pltpu.make_async_copy(
            inputs[kind].at[0, :, cols(jnp.where(first_half, 3328, 0), 512)],
            own.at[kind, 3, :, cols(jnp.where(first_half, 0, 512), 512)],
            piece_sem.at[kind],
        )

    def half_over(kind):
        return pltpu.make_async_remote_copy(
            src_ref=inputs[kind].at[0, :, cols(jnp.where(first_half, 3328, 0), 512)],
            dst_ref=own.at[kind, 3, :, cols(jnp.where(first_half, 0, 512), 512)],
            send_sem=halo_sem.at[0, kind], recv_sem=halo_sem.at[1, kind],
            device_id={"tensor": 3 - t}, device_id_type=MESH,
        )

    def quarter_over(kind):
        return pltpu.make_async_remote_copy(
            src_ref=inputs[kind].at[0, :, cols(jnp.where(first_half, 0, 3584), 256)],
            dst_ref=own.at[kind, 3, :, cols(jnp.where(first_half, 768, 0), 256)],
            send_sem=halo_sem.at[2, kind], recv_sem=halo_sem.at[3, kind],
            device_id={"tensor": jnp.where(first_half, 0, 3)}, device_id_type=MESH,
        )

    def quarter_arrives(kind):
        return pltpu.make_async_remote_copy(
            src_ref=own.at[kind, 3, :, cols(jnp.where(first_half, 768, 0), 256)],
            dst_ref=own.at[kind, 3, :, cols(jnp.where(first_half, 768, 0), 256)],
            send_sem=halo_sem.at[2, kind], recv_sem=halo_sem.at[3, kind],
            device_id={"tensor": jnp.where(first_half, 1, 2)}, device_id_type=MESH,
        )

    @pl.when(inner)
    def _():
        for kind in (0, 1, 2):
            if kind < 2:
                half_over(kind).start()
            quarter_over(kind).start()
            inner_piece(kind).start()

    @pl.when(jnp.logical_not(inner))
    def _():
        for kind in (0, 1, 2):
            outer_piece(kind).start()

    def loaded_whole(kind):
        for slot in range(3):
            loads[3 * kind + slot].wait()

    def loaded_pieces(kind):
        @pl.when(inner)
        def _():
            inner_piece(kind).wait()
            if kind < 2:
                half_over(kind).wait()
            quarter_over(kind).wait_send()

        @pl.when(jnp.logical_not(inner))
        def _():
            outer_piece(kind).wait()
            quarter_arrives(kind).wait_recv()

    def send(number, way, source, target):
        return pltpu.make_async_remote_copy(
            src_ref=source, dst_ref=target,
            send_sem=send_sem.at[number, way], recv_sem=recv_sem.at[number, way],
            device_id=z_device(1 if way == 0 else 3), device_id_type=MESH,
        )

    own_slot = (along(0), along(-1))
    feed_slot = (along(1), along(2))
    behind = (along(-1), along(1))

    both = (0, 1)
    halves = (0, 1)

    def always(copy):
        return copy, None, None

    def wanted(slot, in_first):
        return jnp.logical_or(jnp.logical_or(slot < 3, outer), in_first == first_half)

    def half_wanted(slot, part):
        return jnp.logical_or(
            jnp.logical_or(slot < 3, outer), first_half if part == 0 else jnp.logical_not(first_half)
        )

    def unless(condition, part, device):
        if part == 1:
            return condition
        return jnp.logical_and(condition, jnp.logical_not(jnp.logical_and(outer, z == device)))

    def columns(part):
        return pl.ds(512 * part, 512)

    def feed_roots(way, part):
        copy = send(
            4 + part, way, own.at[2, feed_slot[way], :, columns(part)], roots.at[way, rows(z), columns(part)]
        )
        return (
            copy,
            unless(half_wanted(feed_slot[way], part), part, 1 if way == 0 else 2),
            unless(half_wanted(own_slot[way], part), part, 2 if way == 0 else 1),
        )

    def own_roots(way, part):
        copy = send(
            6 + part, way, own.at[2, own_slot[way], :, columns(part)], roots.at[1 - way, rows(z), columns(part)]
        )
        return copy, half_wanted(own_slot[way], part), half_wanted(own_slot[1 - way], part)

    def roots_on(way, part):
        quarter = rows(behind[way])
        copy = send(
            8 + part, way, roots.at[way, quarter, columns(part)], roots.at[1 - way, quarter, columns(part)]
        )
        return (
            copy,
            unless(half_wanted(own_slot[way], part), part, 2 if way == 0 else 1),
            unless(half_wanted(own_slot[1 - way], part), part, 3 if way == 0 else 0),
        )

    back_slot = (along(-1), along(0))

    def tile_back(step, way):
        quarter = lax.rem(behind[1 - way] + step, RING)
        window = cols(quarter * Q, Q)
        copy = send(9 + step, way, away.at[0, 1 - way, :, window], home.at[0, back_slot[way], :, window])
        return (
            copy,
            wanted(back_slot[way], quarter < 2),
            wanted(feed_slot[1 - way], lax.rem(z + step, RING) < 2),
        )

    def half_back(number, way, kind, part):
        copy = send(
            number + part, way, away.at[kind, 1 - way, :, columns(part)],
            home.at[kind, back_slot[way], :, columns(part)],
        )
        return copy, half_wanted(back_slot[way], part), half_wanted(feed_slot[1 - way], part)

    def detour(number, way, source, target, sender):
        receiver = (sender + 1 if way == 0 else sender + 3) % RING
        return (
            send(number, way, source, target),
            jnp.logical_and(outer, z == sender),
            jnp.logical_and(outer, z == receiver),
        )

    first = columns(0)
    detour_out = [
        detour(17, 0, right_roots.at[0, :, cols(Q * t, 512)], transit, 2),
        detour(17, 1, right_roots.at[0, :, cols(Q * t + 2 * BLK, 512)], transit, 1),
    ]
    detour_over = [
        detour(18, 0, transit, roots.at[0, pl.ds(2 * Q, Q), first], 3),
        detour(18, 1, transit, roots.at[1, pl.ds(Q, Q), first], 0),
    ]
    detour_in = [
        detour(19, 0, roots.at[0, pl.ds(2 * Q, Q), first], roots.at[1, pl.ds(2 * Q, Q), first], 0),
        detour(19, 1, roots.at[1, pl.ds(Q, Q), first], roots.at[0, pl.ds(Q, Q), first], 3),
    ]

    b_feed = [always(send(0, way, own.at[0, feed_slot[way]], blocks.at[way, rows(z)])) for way in both]
    b_own = [always(send(1, way, own.at[0, own_slot[way]], blocks.at[1 - way, rows(z)])) for way in both]
    b_on = [
        always(send(2, way, blocks.at[way, rows(behind[way])], blocks.at[1 - way, rows(behind[way])]))
        for way in both
    ]
    l_feed = [always(send(3, way, own.at[1, feed_slot[way]], other_left.at[way])) for way in both]
    r_feed = [feed_roots(way, part) for part in halves for way in both]
    r_own = [own_roots(way, part) for part in halves for way in both]
    r_on = [roots_on(way, part) for part in halves for way in both]
    back = [
        [tile_back(step, way) for step in (1, 2, 3) for way in both],
        [half_back(13, way, 1, part) for part in halves for way in both],
        [half_back(15, way, 2, part) for part in halves for way in both],
    ]

    def guarded(condition, action):
        if condition is None:
            action()
        else:
            pl.when(condition)(action)

    def start(copies):
        for copy, sends, _ in copies:
            guarded(sends, copy.start)

    def arrive(copies):
        for copy, _, receives in copies:
            guarded(receives, copy.wait_recv)

    def start_where(whole):
        for way in both:
            for copy, slot in ((b_feed[way], feed_slot[way]), (b_own[way], own_slot[way])):
                pl.when((slot < 3) == whole)(copy[0].start)

    start(detour_out)
    loaded_whole(0)
    start_where(True)
    loaded_pieces(0)
    start_where(False)
    loaded_whole(1)
    loaded_pieces(1)
    start(l_feed)
    arrive(detour_out)
    start(detour_over)
    loaded_whole(2)
    loaded_pieces(2)
    start(r_feed)
    for role in both:
        blocks[role, rows(z), :] = own[0, own_slot[role]]
        roots[role, rows(z), :] = own[2, own_slot[role]]
    arrive(b_feed)
    start(b_on)
    start(r_own)
    arrive(b_own)
    arrive(b_on)
    arrive(l_feed)
    arrive(detour_over)
    start(detour_in)

    def compute_stats(role, mine):
        quarter = z if mine else behind[role]
        slot = own_slot[role]
        flipped[...] = blocks[role, :, cols(quarter * Q, Q)].T

        def tile(n, carry):
            window = cols(n * Q, Q)
            left = matmul_nt(blocks[role, rows(quarter), :], blocks[role, rows(n), :])
            left = (left * (1.0 / BLK)).astype(jnp.bfloat16)
            right = matmul(flipped[...], blocks[role, :, window])
            right = (right * (1.0 / BLK)).astype(jnp.bfloat16)
            left_rows = own[1, slot] if mine else other_left[role]
            applied[role, 1 if mine else 0, :, window] = matmul(left_rows, blocks[role, :, window]).astype(jnp.bfloat16)
            if mine:
                home[0, slot, :, window] = left
                home[1, slot, :, window] = right
            else:
                away[0, role, :, window] = left
                away[1, role, :, window] = right
            return carry

        lax.fori_loop(0, 4, tile, 0)

    for way in both:
        feed = own[0, feed_slot[way]]
        tile = (matmul_nt(feed, feed) * (1.0 / BLK)).astype(jnp.bfloat16)
        home[0, feed_slot[way], :, cols(z * Q, Q)] = tile
    arrive(r_feed)
    start(r_on)
    compute_stats(0, False)
    compute_stats(1, False)
    start(back[0])
    compute_stats(0, True)
    compute_stats(1, True)
    arrive(r_own)

    sums[0] = jnp.zeros((8, 128), jnp.float32)

    def compute_update(role, mine, part):
        slot = own_slot[role]

        def tile(n, carry):
            @pl.when(wanted(slot, n < 2))
            def _():
                window = cols(n * Q, Q)
                value = matmul(applied[role, 1 if mine else 0], roots[role, :, window])
                if mine:
                    home[2, slot, :, window] = value.astype(jnp.bfloat16)
                else:
                    away[2, role, :, window] = value.astype(jnp.bfloat16)
                squares = jnp.sum((value * value).reshape(Q // 8, 8, Q), axis=0)
                sums[0] += squares[:, :128] + squares[:, 128:]

            return carry

        lax.fori_loop(2 * part, 2 * part + 2, tile, 0)

    for part in halves:
        arrive(r_on[2 * part : 2 * part + 2])
        if part == 0:
            arrive(detour_in)
        for mine in (False, True):
            for role in both:
                compute_update(role, mine, part)

    def share(stage, number, device):
        return pltpu.make_async_remote_copy(
            src_ref=sums.at[stage], dst_ref=landed.at[number],
            send_sem=sum_sem.at[0, number], recv_sem=sum_sem.at[1, number],
            device_id=device, device_id_type=MESH,
        )

    stages = [
        [(i - 1, z_device(i)) for i in (1, 2, 3)],
        [(i + 2, t_device(i)) for i in (1, 2, 3)],
        [(6, g_device(1))],
        [(7, g_device(2))],
        [(8, g_device(4))],
    ]
    for stage, group in enumerate(stages):
        copies = [share(stage, number, device) for number, device in group]
        for copy in copies:
            copy.start()
        if stage == 0:
            start(back[1])
            start(back[2])
        total = sums[stage]
        for copy in copies:
            copy.wait()
        for number, _ in group:
            total = total + landed[number]
        sums[stage + 1] = total
    square_sum = jnp.sum(sums[len(stages)])
    scale_out[...] = 1.0 / jnp.sqrt(jnp.full((8, 128), square_sum) * (1.0 / (D * FF)) + 1e-06)

    def store(kind, slot):
        return pltpu.make_async_copy(
            home.at[kind, slot], outputs[kind].at[0, :, cols(Q * t + BLK * slot, BLK)], store_sem.at[kind, slot]
        )

    def outer_store(kind):
        return pltpu.make_async_copy(
            home.at[kind, 3, :, cols(jnp.where(first_half, 0, 256), 768)],
            outputs[kind].at[0, :, cols(jnp.where(first_half, 3072, 0), 768)],
            store_sem.at[kind, 3],
        )

    def inner_store(kind):
        return pltpu.make_async_copy(
            home.at[kind, 3, :, cols(jnp.where(first_half, 0, 512), 512)],
            outputs[kind].at[0, :, cols(jnp.where(first_half, 3328, 0), 512)],
            store_sem.at[kind, 3],
        )

    def edge_store(kind):
        return pltpu.make_async_copy(
            edge.at[kind], outputs[kind].at[0, :, cols(jnp.where(first_half, 0, 3584), 256)], store_sem.at[kind, 4]
        )

    def edge_over(kind):
        return pltpu.make_async_remote_copy(
            src_ref=home.at[kind, 3, :, cols(jnp.where(first_half, 768, 0), 256)], dst_ref=edge.at[kind],
            send_sem=edge_sem.at[0, kind], recv_sem=edge_sem.at[1, kind],
            device_id={"tensor": jnp.where(first_half, 1, 2)}, device_id_type=MESH,
        )

    def edge_arrives(kind):
        return pltpu.make_async_remote_copy(
            src_ref=edge.at[kind], dst_ref=edge.at[kind],
            send_sem=edge_sem.at[0, kind], recv_sem=edge_sem.at[1, kind],
            device_id={"tensor": jnp.where(first_half, 0, 3)}, device_id_type=MESH,
        )

    for kind in (0, 1, 2):
        arrive(back[kind])

        @pl.when(jnp.logical_not(inner))
        def _():
            edge_over(kind).start()
            outer_store(kind).start()

        @pl.when(inner)
        def _():
            inner_store(kind).start()

        for slot in range(3):
            store(kind, slot).start()

    for kind in (0, 1, 2):
        @pl.when(inner)
        def _():
            edge_arrives(kind).wait_recv()
            edge_store(kind).start()

    for kind in (0, 1, 2):
        for slot in range(3):
            store(kind, slot).wait()

        @pl.when(inner)
        def _():
            inner_store(kind).wait()
            edge_store(kind).wait()

        @pl.when(jnp.logical_not(inner))
        def _():
            outer_store(kind).wait()
            edge_over(kind).wait_send()

    for copies in [b_feed, b_own, b_on, l_feed, r_feed, r_own, r_on, detour_out, detour_over, detour_in] + back:
        for copy, sends, _ in copies:
            guarded(sends, copy.wait_send)


def shards(grad, left_roots, right_roots):
    half = jnp.bfloat16
    out = jax.ShapeDtypeStruct((1, Q, COLS), half)
    hbm = pl.BlockSpec(memory_space=pl.ANY)
    dma = pltpu.SemaphoreType.DMA
    left, right, update, scale = pl.pallas_call(
        kernel,
        out_shape=[out, out, out, jax.ShapeDtypeStruct((8, 128), jnp.float32)],
        in_specs=[pl.BlockSpec(memory_space=pltpu.HBM)] * 3,
        out_specs=[hbm] * 3 + [pl.BlockSpec(memory_space=pltpu.VMEM)],
        scratch_shapes=[
            pltpu.VMEM((3, 4, Q, BLK), half),
            pltpu.VMEM((2, BLK, BLK), half),
            pltpu.VMEM((2, BLK, BLK), half),
            pltpu.VMEM((2, Q, BLK), half),
            pltpu.VMEM((Q, BLK), half),
            pltpu.VMEM((2, 2, Q, BLK), half),
            pltpu.VMEM((3, 2, Q, BLK), half),
            pltpu.VMEM((3, 4, Q, BLK), half),
            pltpu.VMEM((3, Q, Q), half),
            pltpu.VMEM((Q, 512), half),
            pltpu.VMEM((6, 8, 128), jnp.float32),
            pltpu.VMEM((9, 8, 128), jnp.float32),
            dma((3, 3)), dma((3,)), dma((4, 3)), dma((20, 2)), dma((20, 2)), dma((2, 9)), dma((3, 5)), dma((2, 3)),
        ],
        compiler_params=pltpu.CompilerParams(
            collective_id=0, has_side_effects=True, vmem_limit_bytes=30 * 1024 * 1024
        ),
        cost_estimate=pl.CostEstimate(flops=8_600_000_000, bytes_accessed=12_000_000, transcendentals=0),
    )(*[pltpu.with_memory_space_constraint(a, pltpu.HBM) for a in (grad, left_roots, right_roots)])
    return finish(left, right, update, scale)


def finish_kernel(left, right, update, scale, left_out, right_out, update_out, wide, narrow, sem):
    part = 64
    copies = []
    slot = 0
    for start in range(0, Q, part):
        rows = pl.ds(start, part)
        for source, target in ((left, left_out), (right, right_out)):
            wide[slot] = source[0, rows, :].astype(jnp.float32)
            copies.append(pltpu.make_async_copy(wide.at[slot], target.at[0, rows, :], sem.at[len(copies)]))
            copies[-1].start()
            slot += 1
        narrow[rows, :] = (update[0, rows, :].astype(jnp.float32) * scale[0:1, 0:1]).astype(jnp.bfloat16)
        copies.append(pltpu.make_async_copy(narrow.at[rows, :], update_out.at[0, rows, :], sem.at[len(copies)]))
        copies[-1].start()
    for copy in copies:
        copy.wait()


def finish(left, right, update, scale):
    shape = (1, Q, COLS)
    return tuple(pl.pallas_call(
        finish_kernel,
        out_shape=[jax.ShapeDtypeStruct(shape, d) for d in (jnp.float32, jnp.float32, jnp.bfloat16)],
        in_specs=[pl.BlockSpec(memory_space=pltpu.VMEM)] * 4,
        out_specs=[pl.BlockSpec(memory_space=pl.ANY)] * 3,
        scratch_shapes=[
            pltpu.VMEM((8, 64, COLS), jnp.float32), pltpu.VMEM((Q, COLS), jnp.bfloat16), pltpu.SemaphoreType.DMA((12,))
        ],
        compiler_params=pltpu.CompilerParams(vmem_limit_bytes=16 * 1024 * 1024),
    )(left, right, update, scale))


def solution(mesh):
    spec = P(None, "fsdp", "tensor")
    return jax.shard_map(shards, mesh=mesh, in_specs=(spec,) * 3, out_specs=(spec,) * 3, check_vma=False)
```

```python
import functools

import jax
import jax.numpy as jnp
from jax import lax
from jax.experimental import pallas as pl
from jax.experimental.pallas import tpu as pltpu
from jax.sharding import PartitionSpec as P

D = 8192
FF = 15360
BLK = 1024
Q = 256
RING = 4
COLS = 3840
TURN = 0
MESH = pl.DeviceIdType.MESH


def matmul(a, b):
    return lax.dot_general(a, b, (((1,), (0,)), ((), ())), preferred_element_type=jnp.float32)


def matmul_nt(a, b):
    return lax.dot_general(a, b, (((1,), (1,)), ((), ())), preferred_element_type=jnp.float32)


def kernel(
    grad, left_roots, right_roots, left_out, right_out, update_out, scale_out,
    own, blocks, roots, other_left, flipped, applied, away, home, edge, transit, sums, landed,
    load_sem, piece_sem, halo_sem, swap_sem, send_sem, recv_sem, sum_sem, store_sem, edge_sem,
):
    inputs = (grad, left_roots, right_roots)
    outputs = (left_out, right_out, update_out)
    t = lax.axis_index("tensor")
    f = lax.axis_index("fsdp")
    z = lax.rem(f, RING)
    g = lax.div(f, RING)
    inner = jnp.logical_or(t == 1, t == 2)
    outer = jnp.logical_not(inner)
    first_half = t < 2

    def along(step):
        return lax.rem(z + step + RING, RING)

    def z_device(step):
        return {"fsdp": g * RING + along(step)}

    def t_device(step):
        return {"tensor": lax.rem(t + step, 4)}

    def g_device(bit):
        other = g + bit - 2 * bit * lax.rem(lax.div(g, bit), 2)
        return {"fsdp": other * RING + z}

    def rows(quarter):
        return pl.ds(pl.multiple_of(quarter * Q, Q), Q)

    def cols(start, size):
        return pl.ds(pl.multiple_of(start, Q), size)

    loads = []
    for kind in (0, 1, 2):
        for slot in range(3):
            loads.append(pltpu.make_async_copy(
                inputs[kind].at[0, :, cols(Q * t + BLK * slot, BLK)], own.at[kind, slot], load_sem.at[kind, slot]
            ))
    for copy in loads:
        copy.start()

    barrier = pltpu.get_barrier_semaphore()
    partners = [z_device(i) for i in (1, 2, 3)] + [t_device(i) for i in (1, 2, 3)] + [g_device(b) for b in (1, 2, 4)]
    for device in partners:
        pl.semaphore_signal(barrier, inc=1, device_id=device, device_id_type=MESH)
    pl.semaphore_wait(barrier, len(partners))

    def outer_piece(kind):
        return pltpu.make_async_copy(
            inputs[kind].at[0, :, cols(jnp.where(first_half, 3072, 0), 768)],
            own.at[kind, 3, :, cols(jnp.where(first_half, 0, 256), 768)],
            piece_sem.at[kind],
        )

    def inner_piece(kind):
        return pltpu.make_async_copy(
            inputs[kind].at[0, :, cols(jnp.where(first_half, 3328, 0), 512)],
            own.at[kind, 3, :, cols(jnp.where(first_half, 0, 512), 512)],
            piece_sem.at[kind],
        )

    def half_over(kind):
        return pltpu.make_async_remote_copy(
            src_ref=inputs[kind].at[0, :, cols(jnp.where(first_half, 3328, 0), 512)],
            dst_ref=own.at[kind, 3, :, cols(jnp.where(first_half, 0, 512), 512)],
            send_sem=halo_sem.at[0, kind], recv_sem=halo_sem.at[1, kind],
            device_id={"tensor": 3 - t}, device_id_type=MESH,
        )

    def quarter_over(kind):
        return pltpu.make_async_remote_copy(
            src_ref=inputs[kind].at[0, :, cols(jnp.where(first_half, 0, 3584), 256)],
            dst_ref=own.at[kind, 3, :, cols(jnp.where(first_half, 768, 0), 256)],
            send_sem=halo_sem.at[2, kind], recv_sem=halo_sem.at[3, kind],
            device_id={"tensor": jnp.where(first_half, 0, 3)}, device_id_type=MESH,
        )

    def quarter_arrives(kind):
        return pltpu.make_async_remote_copy(
            src_ref=own.at[kind, 3, :, cols(jnp.where(first_half, 768, 0), 256)],
            dst_ref=own.at[kind, 3, :, cols(jnp.where(first_half, 768, 0), 256)],
            send_sem=halo_sem.at[2, kind], recv_sem=halo_sem.at[3, kind],
            device_id={"tensor": jnp.where(first_half, 1, 2)}, device_id_type=MESH,
        )

    @pl.when(inner)
    def _():
        for kind in (0, 1, 2):
            if kind < 2:
                half_over(kind).start()
            quarter_over(kind).start()
            inner_piece(kind).start()

    @pl.when(jnp.logical_not(inner))
    def _():
        for kind in (0, 1, 2):
            outer_piece(kind).start()

    def loaded_whole(kind):
        for slot in range(3):
            loads[3 * kind + slot].wait()

    def loaded_pieces(kind):
        @pl.when(inner)
        def _():
            inner_piece(kind).wait()
            quarter_over(kind).wait_send()

        @pl.when(outer)
        def _():
            outer_piece(kind).wait()
            quarter_arrives(kind).wait_recv()

    def loaded_half(kind):
        pl.when(inner)(half_over(kind).wait)

    def send(number, way, source, target):
        return pltpu.make_async_remote_copy(
            src_ref=source, dst_ref=target,
            send_sem=send_sem.at[number, way], recv_sem=recv_sem.at[number, way],
            device_id=z_device(1 if way == 0 else 3), device_id_type=MESH,
        )

    own_slot = (along(-TURN), along(-TURN - 1))
    feed_slot = (along(1 - TURN), along(2 - TURN))
    behind = (along(-1), along(1))

    both = (0, 1)
    halves = (0, 1)

    def wanted(slot, in_first):
        return jnp.logical_or(jnp.logical_or(slot < 3, outer), in_first == first_half)

    def half_wanted(slot, part):
        return jnp.logical_or(
            jnp.logical_or(slot < 3, outer), first_half if part == 0 else jnp.logical_not(first_half)
        )

    def unless(condition, part, device):
        if part == 1 or device is None:
            return condition
        return jnp.logical_and(condition, jnp.logical_not(jnp.logical_and(outer, z == (device + TURN) % RING)))

    def columns(part):
        return pl.ds(512 * part, 512)

    def feed_to(number, way, part, source, target, skipped=(None, None)):
        copy = send(number + part, way, source.at[feed_slot[way], :, columns(part)], target.at[:, columns(part)])
        return (
            copy,
            unless(half_wanted(feed_slot[way], part), part, skipped[way]),
            unless(half_wanted(own_slot[way], part), part, skipped[1 - way]),
        )

    def own_to(number, way, part, source, full):
        copy = send(
            number + part, way, source.at[own_slot[way], :, columns(part)],
            full.at[1 - way, rows(z), columns(part)],
        )
        return copy, half_wanted(own_slot[way], part), half_wanted(own_slot[1 - way], part)

    def pass_on(number, way, part, full, skipped=((None, None), (None, None))):
        quarter = rows(behind[way])
        copy = send(
            number + part, way, full.at[way, quarter, columns(part)], full.at[1 - way, quarter, columns(part)]
        )
        return (
            copy,
            unless(half_wanted(own_slot[way], part), part, skipped[0][way]),
            unless(half_wanted(own_slot[1 - way], part), part, skipped[1][way]),
        )

    back_slot = (own_slot[1], own_slot[0])

    def tile_back(step, way):
        quarter = lax.rem(behind[1 - way] + step, RING)
        window = cols(quarter * Q, Q)
        copy = send(13 + step, way, away.at[0, 1 - way, :, window], home.at[0, back_slot[way], :, window])
        return (
            copy,
            wanted(back_slot[way], quarter < 2),
            wanted(feed_slot[1 - way], lax.rem(z + step, RING) < 2),
        )

    def half_back(number, way, kind, part):
        copy = send(
            number + part, way, away.at[kind, 1 - way, :, columns(part)],
            home.at[kind, back_slot[way], :, columns(part)],
        )
        return copy, half_wanted(back_slot[way], part), half_wanted(feed_slot[1 - way], part)

    def detour(number, way, source, target, sender):
        sender = (sender + TURN) % RING
        receiver = (sender + 1 if way == 0 else sender + 3) % RING
        return (
            send(number, way, source, target),
            jnp.logical_and(outer, z == sender),
            jnp.logical_and(outer, z == receiver),
        )

    first = columns(0)
    low = pl.ds((1 + TURN) % RING * Q, Q)
    high = pl.ds((2 + TURN) % RING * Q, Q)
    detour_out = [
        detour(21, 0, right_roots.at[0, :, cols(Q * t, 512)], transit, 2),
        detour(21, 1, right_roots.at[0, :, cols(Q * t + 2 * BLK, 512)], transit, 1),
    ]
    detour_over = [
        detour(22, 0, transit, roots.at[0, high, first], 3),
        detour(22, 1, transit, roots.at[1, low, first], 0),
    ]
    detour_in = [
        detour(23, 0, roots.at[0, high, first], roots.at[1, high, first], 0),
        detour(23, 1, roots.at[1, low, first], roots.at[0, low, first], 3),
    ]

    each = [(way, part) for part in halves for way in both]
    b_feed = [feed_to(0, way, part, own.at[0], blocks.at[way, rows(z)]) for way, part in each]
    b_own = [own_to(2, way, part, own.at[0], blocks) for way, part in each]
    b_on = [pass_on(4, way, part, blocks) for way, part in each]
    l_feed = [feed_to(6, way, part, own.at[1], other_left.at[way]) for way, part in each]
    r_feed = [feed_to(8, way, part, own.at[2], roots.at[way, rows(z)], (1, 2)) for way, part in each]
    r_own = [own_to(10, way, part, own.at[2], roots) for way, part in each]
    r_on = [pass_on(12, way, part, roots, ((2, 1), (3, 0))) for way, part in each]
    back = [
        [tile_back(step, way) for step in (1, 2, 3) for way in both],
        [half_back(17, way, 1, part) for way, part in each],
        [half_back(19, way, 2, part) for way, part in each],
    ]

    swap_role = jnp.where(own_slot[0] == 3, 0, 1)
    swaps = jnp.logical_and(inner, jnp.logical_or(own_slot[0] == 3, own_slot[1] == 3))
    own_half = pl.ds(pl.multiple_of(jnp.where(first_half, 0, 512), 512), 512)

    def swap(number, ref):
        return pltpu.make_async_remote_copy(
            src_ref=ref, dst_ref=ref, send_sem=swap_sem.at[0, number], recv_sem=swap_sem.at[1, number],
            device_id={"tensor": 3 - t}, device_id_type=MESH,
        )

    swap_grad = [swap(step - 1, blocks.at[swap_role, rows(along(step)), own_half]) for step in (1, 2, 3)]
    swap_left = swap(3, other_left.at[swap_role, :, own_half])

    def guarded(condition, action):
        if condition is None:
            action()
        else:
            pl.when(condition)(action)

    def start(copies):
        for copy, sends, _ in copies:
            guarded(sends, copy.start)

    def arrive(copies):
        for copy, _, receives in copies:
            guarded(receives, copy.wait_recv)

    def start_where(whole):
        for copies, slots in ((b_feed, feed_slot), (b_own, own_slot)):
            for (copy, sends, _), (way, _) in zip(copies, each):
                pl.when(jnp.logical_and(sends, (slots[way] < 3) == whole))(copy.start)

    start(detour_out)
    loaded_whole(0)
    start_where(True)
    loaded_pieces(0)
    start_where(False)
    loaded_whole(1)
    loaded_pieces(1)
    start(l_feed)
    arrive(detour_out)
    start(detour_over)
    loaded_whole(2)
    loaded_pieces(2)
    start(r_feed)
    loaded_half(0)
    loaded_half(1)
    for role in both:
        blocks[role, rows(z), :] = own[0, own_slot[role]]
        roots[role, rows(z), :] = own[2, own_slot[role]]
    arrive(b_feed)
    start(b_on)
    start(r_own)
    arrive(b_own)

    @pl.when(swaps)
    def _():
        swap_grad[0].start()
        swap_grad[2].start()

    arrive(l_feed)
    pl.when(swaps)(swap_left.start)
    arrive(b_on)
    pl.when(swaps)(swap_grad[1].start)
    arrive(detour_over)
    start(detour_in)
    arrive(r_feed)
    start(r_on)

    @pl.when(swaps)
    def _():
        for copy in swap_grad + [swap_left]:
            copy.wait()

    def compute_stats(role, mine):
        quarter = z if mine else behind[role]
        slot = own_slot[role]
        flipped[...] = blocks[role, :, cols(quarter * Q, Q)].T

        def tile(n, carry):
            window = cols(n * Q, Q)
            left = matmul_nt(blocks[role, rows(quarter), :], blocks[role, rows(n), :])
            left = (left * (1.0 / BLK)).astype(jnp.bfloat16)
            right = matmul(flipped[...], blocks[role, :, window])
            right = (right * (1.0 / BLK)).astype(jnp.bfloat16)
            if mine:
                home[0, slot, :, window] = left
                home[1, slot, :, window] = right
            else:
                away[0, role, :, window] = left
                away[1, role, :, window] = right
            return carry

        lax.fori_loop(0, 4, tile, 0)

    def compute_diagonal():
        for way in both:
            feed = own[0, feed_slot[way]]
            tile = (matmul_nt(feed, feed) * (1.0 / BLK)).astype(jnp.bfloat16)
            home[0, feed_slot[way], :, cols(z * Q, Q)] = tile

    def compute_applied(role, mine):
        def tile(n, carry):
            window = cols(n * Q, Q)
            left_rows = own[1, own_slot[role]] if mine else other_left[role]
            applied[role, 1 if mine else 0, :, window] = matmul(left_rows, blocks[role, :, window]).astype(jnp.bfloat16)
            return carry

        lax.fori_loop(0, 4, tile, 0)

    compute_stats(0, False)
    compute_stats(1, False)
    start(back[0])
    for mine in (False, True):
        for role in both:
            compute_applied(role, mine)
    compute_diagonal()
    compute_stats(0, True)
    compute_stats(1, True)
    arrive(r_own)

    sums[0] = jnp.zeros((8, 128), jnp.float32)

    def compute_update(role, mine, part):
        slot = own_slot[role]

        def tile(n, carry):
            @pl.when(wanted(slot, n < 2))
            def _():
                window = cols(n * Q, Q)
                value = matmul(applied[role, 1 if mine else 0], roots[role, :, window])
                if mine:
                    home[2, slot, :, window] = value.astype(jnp.bfloat16)
                else:
                    away[2, role, :, window] = value.astype(jnp.bfloat16)
                squares = jnp.sum((value * value).reshape(Q // 8, 8, Q), axis=0)
                sums[0] += squares[:, :128] + squares[:, 128:]

            return carry

        lax.fori_loop(2 * part, 2 * part + 2, tile, 0)

    for part in halves:
        arrive(r_on[2 * part : 2 * part + 2])
        if part == 0:
            arrive(detour_in)
        for mine in (False, True):
            for role in both:
                compute_update(role, mine, part)

    def share(stage, number, device):
        return pltpu.make_async_remote_copy(
            src_ref=sums.at[stage], dst_ref=landed.at[number],
            send_sem=sum_sem.at[0, number], recv_sem=sum_sem.at[1, number],
            device_id=device, device_id_type=MESH,
        )

    stages = [
        [(i - 1, z_device(i)) for i in (1, 2, 3)],
        [(i + 2, t_device(i)) for i in (1, 2, 3)],
        [(6, g_device(1))],
        [(7, g_device(2))],
        [(8, g_device(4))],
    ]
    for stage, group in enumerate(stages):
        copies = [share(stage, number, device) for number, device in group]
        for copy in copies:
            copy.start()
        if stage == 0:
            start(back[1])
            pl.when(t == 0)(lambda: start(back[2][2:] + back[2][:2]))
            pl.when(t > 0)(lambda: start(back[2]))
        total = sums[stage]
        for copy in copies:
            copy.wait()
        for number, _ in group:
            total = total + landed[number]
        sums[stage + 1] = total
    square_sum = jnp.sum(sums[len(stages)])
    scale_out[...] = 1.0 / jnp.sqrt(jnp.full((8, 128), square_sum) * (1.0 / (D * FF)) + 1e-06)

    def store(kind, slot):
        return pltpu.make_async_copy(
            home.at[kind, slot], outputs[kind].at[0, :, cols(Q * t + BLK * slot, BLK)], store_sem.at[kind, slot]
        )

    def outer_store(kind):
        return pltpu.make_async_copy(
            home.at[kind, 3, :, cols(jnp.where(first_half, 0, 256), 768)],
            outputs[kind].at[0, :, cols(jnp.where(first_half, 3072, 0), 768)],
            store_sem.at[kind, 3],
        )

    def inner_store(kind):
        return pltpu.make_async_copy(
            home.at[kind, 3, :, cols(jnp.where(first_half, 0, 512), 512)],
            outputs[kind].at[0, :, cols(jnp.where(first_half, 3328, 0), 512)],
            store_sem.at[kind, 3],
        )

    def edge_store(kind):
        return pltpu.make_async_copy(
            edge.at[kind], outputs[kind].at[0, :, cols(jnp.where(first_half, 0, 3584), 256)], store_sem.at[kind, 4]
        )

    def edge_over(kind):
        return pltpu.make_async_remote_copy(
            src_ref=home.at[kind, 3, :, cols(jnp.where(first_half, 768, 0), 256)], dst_ref=edge.at[kind],
            send_sem=edge_sem.at[0, kind], recv_sem=edge_sem.at[1, kind],
            device_id={"tensor": jnp.where(first_half, 1, 2)}, device_id_type=MESH,
        )

    def edge_arrives(kind):
        return pltpu.make_async_remote_copy(
            src_ref=edge.at[kind], dst_ref=edge.at[kind],
            send_sem=edge_sem.at[0, kind], recv_sem=edge_sem.at[1, kind],
            device_id={"tensor": jnp.where(first_half, 0, 3)}, device_id_type=MESH,
        )

    for kind in (0, 1, 2):
        if kind < 2:
            arrive(back[kind])
            pl.when(outer)(edge_over(kind).start)
        else:
            @pl.when(t == 0)
            def _():
                arrive(back[2][2:])
                edge_over(2).start()
                arrive(back[2][:2])

            @pl.when(t > 0)
            def _():
                arrive(back[2][:2])
                pl.when(outer)(edge_over(2).start)
                arrive(back[2][2:])

        @pl.when(outer)
        def _():
            outer_store(kind).start()

        @pl.when(inner)
        def _():
            inner_store(kind).start()

        for slot in range(3):
            store(kind, slot).start()

    for kind in (0, 1, 2):
        @pl.when(inner)
        def _():
            edge_arrives(kind).wait_recv()
            edge_store(kind).start()

    for kind in (0, 1, 2):
        for slot in range(3):
            store(kind, slot).wait()

        @pl.when(inner)
        def _():
            inner_store(kind).wait()
            edge_store(kind).wait()

        @pl.when(jnp.logical_not(inner))
        def _():
            outer_store(kind).wait()
            edge_over(kind).wait_send()

    for copies in [b_feed, b_own, b_on, l_feed, r_feed, r_own, r_on, detour_out, detour_over, detour_in] + back:
        for copy, sends, _ in copies:
            guarded(sends, copy.wait_send)


def shards(grad, left_roots, right_roots):
    half = jnp.bfloat16
    out = jax.ShapeDtypeStruct((1, Q, COLS), half)
    hbm = pl.BlockSpec(memory_space=pl.ANY)
    dma = pltpu.SemaphoreType.DMA
    left, right, update, scale = pl.pallas_call(
        kernel,
        out_shape=[out, out, out, jax.ShapeDtypeStruct((8, 128), jnp.float32)],
        in_specs=[pl.BlockSpec(memory_space=pltpu.HBM)] * 3,
        out_specs=[hbm] * 3 + [pl.BlockSpec(memory_space=pltpu.VMEM)],
        scratch_shapes=[
            pltpu.VMEM((3, 4, Q, BLK), half),
            pltpu.VMEM((2, BLK, BLK), half),
            pltpu.VMEM((2, BLK, BLK), half),
            pltpu.VMEM((2, Q, BLK), half),
            pltpu.VMEM((Q, BLK), half),
            pltpu.VMEM((2, 2, Q, BLK), half),
            pltpu.VMEM((3, 2, Q, BLK), half),
            pltpu.VMEM((3, 4, Q, BLK), half),
            pltpu.VMEM((3, Q, Q), half),
            pltpu.VMEM((Q, 512), half),
            pltpu.VMEM((6, 8, 128), jnp.float32),
            pltpu.VMEM((9, 8, 128), jnp.float32),
            dma((3, 3)), dma((3,)), dma((4, 3)), dma((2, 4)), dma((24, 2)), dma((24, 2)), dma((2, 9)), dma((3, 5)), dma((2, 3)),
        ],
        compiler_params=pltpu.CompilerParams(
            collective_id=0, has_side_effects=True, vmem_limit_bytes=30 * 1024 * 1024
        ),
        cost_estimate=pl.CostEstimate(flops=8_600_000_000, bytes_accessed=12_000_000, transcendentals=0),
    )(*[pltpu.with_memory_space_constraint(a, pltpu.HBM) for a in (grad, left_roots, right_roots)])
    return finish(left, right, update, scale)


def finish_kernel(left, right, update, scale, left_out, right_out, update_out, wide, narrow, sem):
    part = 64
    copies = []
    slot = 0
    for start in range(0, Q, part):
        rows = pl.ds(start, part)
        for source, target in ((left, left_out), (right, right_out)):
            wide[slot] = source[0, rows, :].astype(jnp.float32)
            copies.append(pltpu.make_async_copy(wide.at[slot], target.at[0, rows, :], sem.at[len(copies)]))
            copies[-1].start()
            slot += 1
        narrow[rows, :] = (update[0, rows, :].astype(jnp.float32) * scale[0:1, 0:1]).astype(jnp.bfloat16)
        copies.append(pltpu.make_async_copy(narrow.at[rows, :], update_out.at[0, rows, :], sem.at[len(copies)]))
        copies[-1].start()
    for copy in copies:
        copy.wait()


def finish(left, right, update, scale):
    shape = (1, Q, COLS)
    return tuple(pl.pallas_call(
        finish_kernel,
        out_shape=[jax.ShapeDtypeStruct(shape, d) for d in (jnp.float32, jnp.float32, jnp.bfloat16)],
        in_specs=[pl.BlockSpec(memory_space=pltpu.VMEM)] * 4,
        out_specs=[pl.BlockSpec(memory_space=pl.ANY)] * 3,
        scratch_shapes=[
            pltpu.VMEM((8, 64, COLS), jnp.float32), pltpu.VMEM((Q, COLS), jnp.bfloat16), pltpu.SemaphoreType.DMA((12,))
        ],
        compiler_params=pltpu.CompilerParams(vmem_limit_bytes=16 * 1024 * 1024),
    )(left, right, update, scale))


def solution(mesh):
    spec = P(None, "fsdp", "tensor")
    return jax.shard_map(shards, mesh=mesh, in_specs=(spec,) * 3, out_specs=(spec,) * 3, check_vma=False)
```

```python
import functools

import jax
import jax.numpy as jnp
from jax import lax
from jax.experimental import pallas as pl
from jax.experimental.pallas import tpu as pltpu
from jax.sharding import PartitionSpec as P

D = 8192
FF = 15360
BLK = 1024
Q = 256
RING = 4
COLS = 3840
TURN = 0
MESH = pl.DeviceIdType.MESH


def matmul(a, b):
    return lax.dot_general(a, b, (((1,), (0,)), ((), ())), preferred_element_type=jnp.float32)


def matmul_nt(a, b):
    return lax.dot_general(a, b, (((1,), (1,)), ((), ())), preferred_element_type=jnp.float32)


def kernel(
    grad, left_roots, right_roots, left_out, right_out, update_out, scale_out,
    own, blocks, roots, other_left, flipped, applied, away, home, edge, transit, sums, landed,
    load_sem, piece_sem, halo_sem, swap_sem, send_sem, recv_sem, sum_sem, store_sem, edge_sem,
):
    inputs = (grad, left_roots, right_roots)
    outputs = (left_out, right_out, update_out)
    t = lax.axis_index("tensor")
    f = lax.axis_index("fsdp")
    z = lax.rem(f, RING)
    g = lax.div(f, RING)
    inner = jnp.logical_or(t == 1, t == 2)
    outer = jnp.logical_not(inner)
    detours = lax.rem(t, 2) == 0
    first_half = t < 2

    def along(step):
        return lax.rem(z + step + RING, RING)

    def z_device(step):
        return {"fsdp": g * RING + along(step)}

    def t_device(step):
        return {"tensor": lax.rem(t + step, 4)}

    def g_device(bit):
        other = g + bit - 2 * bit * lax.rem(lax.div(g, bit), 2)
        return {"fsdp": other * RING + z}

    def rows(quarter):
        return pl.ds(pl.multiple_of(quarter * Q, Q), Q)

    def cols(start, size):
        return pl.ds(pl.multiple_of(start, Q), size)

    loads = []
    for kind in (0, 1, 2):
        for slot in range(3):
            loads.append(pltpu.make_async_copy(
                inputs[kind].at[0, :, cols(Q * t + BLK * slot, BLK)], own.at[kind, slot], load_sem.at[kind, slot]
            ))
    for copy in loads:
        copy.start()

    barrier = pltpu.get_barrier_semaphore()
    partners = [z_device(i) for i in (1, 2, 3)] + [t_device(i) for i in (1, 2, 3)] + [g_device(b) for b in (1, 2, 4)]
    for device in partners:
        pl.semaphore_signal(barrier, inc=1, device_id=device, device_id_type=MESH)
    pl.semaphore_wait(barrier, len(partners))

    def outer_piece(kind):
        return pltpu.make_async_copy(
            inputs[kind].at[0, :, cols(jnp.where(first_half, 3072, 0), 768)],
            own.at[kind, 3, :, cols(jnp.where(first_half, 0, 256), 768)],
            piece_sem.at[kind],
        )

    def inner_piece(kind):
        return pltpu.make_async_copy(
            inputs[kind].at[0, :, cols(jnp.where(first_half, 3328, 0), 512)],
            own.at[kind, 3, :, cols(jnp.where(first_half, 0, 512), 512)],
            piece_sem.at[kind],
        )

    def half_over(kind):
        return pltpu.make_async_remote_copy(
            src_ref=inputs[kind].at[0, :, cols(jnp.where(first_half, 3328, 0), 512)],
            dst_ref=own.at[kind, 3, :, cols(jnp.where(first_half, 0, 512), 512)],
            send_sem=halo_sem.at[0, kind], recv_sem=halo_sem.at[1, kind],
            device_id={"tensor": 3 - t}, device_id_type=MESH,
        )

    def quarter_over(kind):
        return pltpu.make_async_remote_copy(
            src_ref=inputs[kind].at[0, :, cols(jnp.where(first_half, 0, 3584), 256)],
            dst_ref=own.at[kind, 3, :, cols(jnp.where(first_half, 768, 0), 256)],
            send_sem=halo_sem.at[2, kind], recv_sem=halo_sem.at[3, kind],
            device_id={"tensor": jnp.where(first_half, 0, 3)}, device_id_type=MESH,
        )

    def quarter_arrives(kind):
        return pltpu.make_async_remote_copy(
            src_ref=own.at[kind, 3, :, cols(jnp.where(first_half, 768, 0), 256)],
            dst_ref=own.at[kind, 3, :, cols(jnp.where(first_half, 768, 0), 256)],
            send_sem=halo_sem.at[2, kind], recv_sem=halo_sem.at[3, kind],
            device_id={"tensor": jnp.where(first_half, 1, 2)}, device_id_type=MESH,
        )

    @pl.when(inner)
    def _():
        for kind in (0, 1, 2):
            if kind < 2:
                half_over(kind).start()
            quarter_over(kind).start()
            inner_piece(kind).start()

    @pl.when(jnp.logical_not(inner))
    def _():
        for kind in (0, 1, 2):
            outer_piece(kind).start()

    def loaded_whole(kind):
        for slot in range(3):
            loads[3 * kind + slot].wait()

    def loaded_pieces(kind):
        @pl.when(inner)
        def _():
            inner_piece(kind).wait()
            quarter_over(kind).wait_send()

        @pl.when(outer)
        def _():
            outer_piece(kind).wait()
            quarter_arrives(kind).wait_recv()

    def loaded_half(kind):
        pl.when(inner)(half_over(kind).wait)

    def send(number, way, source, target):
        return pltpu.make_async_remote_copy(
            src_ref=source, dst_ref=target,
            send_sem=send_sem.at[number, way], recv_sem=recv_sem.at[number, way],
            device_id=z_device(1 if way == 0 else 3), device_id_type=MESH,
        )

    own_slot = (along(-TURN), along(-TURN - 1))
    feed_slot = (along(1 - TURN), along(2 - TURN))
    behind = (along(-1), along(1))

    both = (0, 1)
    halves = (0, 1)

    def wanted(slot, in_first):
        return jnp.logical_or(jnp.logical_or(slot < 3, outer), in_first == first_half)

    def half_wanted(slot, part):
        return jnp.logical_or(
            jnp.logical_or(slot < 3, outer), first_half if part == 0 else jnp.logical_not(first_half)
        )

    def unless(condition, part, device):
        if part == 1 or device is None:
            return condition
        return jnp.logical_and(condition, jnp.logical_not(jnp.logical_and(detours, z == (device + TURN) % RING)))

    def columns(part):
        return pl.ds(512 * part, 512)

    def feed_to(number, way, part, source, target, skipped=(None, None)):
        copy = send(number + part, way, source.at[feed_slot[way], :, columns(part)], target.at[:, columns(part)])
        return (
            copy,
            unless(half_wanted(feed_slot[way], part), part, skipped[way]),
            unless(half_wanted(own_slot[way], part), part, skipped[1 - way]),
        )

    def own_to(number, way, part, source, full):
        copy = send(
            number + part, way, source.at[own_slot[way], :, columns(part)],
            full.at[1 - way, rows(z), columns(part)],
        )
        return copy, half_wanted(own_slot[way], part), half_wanted(own_slot[1 - way], part)

    def pass_on(number, way, part, full, skipped=((None, None), (None, None))):
        quarter = rows(behind[way])
        copy = send(
            number + part, way, full.at[way, quarter, columns(part)], full.at[1 - way, quarter, columns(part)]
        )
        return (
            copy,
            unless(half_wanted(own_slot[way], part), part, skipped[0][way]),
            unless(half_wanted(own_slot[1 - way], part), part, skipped[1][way]),
        )

    back_slot = (own_slot[1], own_slot[0])

    def tile_back(step, way):
        quarter = lax.rem(behind[1 - way] + step, RING)
        window = cols(quarter * Q, Q)
        copy = send(13 + step, way, away.at[0, 1 - way, :, window], home.at[0, back_slot[way], :, window])
        return (
            copy,
            wanted(back_slot[way], quarter < 2),
            wanted(feed_slot[1 - way], lax.rem(z + step, RING) < 2),
        )

    def half_back(number, way, kind, part):
        copy = send(
            number + part, way, away.at[kind, 1 - way, :, columns(part)],
            home.at[kind, back_slot[way], :, columns(part)],
        )
        return copy, half_wanted(back_slot[way], part), half_wanted(feed_slot[1 - way], part)

    def detour(number, way, source, target, sender):
        sender = (sender + TURN) % RING
        receiver = (sender + 1 if way == 0 else sender + 3) % RING
        return (
            send(number, way, source, target),
            jnp.logical_and(detours, z == sender),
            jnp.logical_and(detours, z == receiver),
        )

    first = columns(0)
    low = pl.ds((1 + TURN) % RING * Q, Q)
    high = pl.ds((2 + TURN) % RING * Q, Q)
    detour_out = [
        detour(21, 0, right_roots.at[0, :, cols(Q * t, 512)], transit, 2),
        detour(21, 1, right_roots.at[0, :, cols(Q * t + 2 * BLK, 512)], transit, 1),
    ]
    detour_over = [
        detour(22, 0, transit, roots.at[0, high, first], 3),
        detour(22, 1, transit, roots.at[1, low, first], 0),
    ]
    detour_in = [
        detour(23, 0, roots.at[0, high, first], roots.at[1, high, first], 0),
        detour(23, 1, roots.at[1, low, first], roots.at[0, low, first], 3),
    ]

    each = [(way, part) for part in halves for way in both]
    b_feed = [feed_to(0, way, part, own.at[0], blocks.at[way, rows(z)]) for way, part in each]
    b_own = [own_to(2, way, part, own.at[0], blocks) for way, part in each]
    b_on = [pass_on(4, way, part, blocks) for way, part in each]
    l_feed = [feed_to(6, way, part, own.at[1], other_left.at[way]) for way, part in each]
    r_feed = [feed_to(8, way, part, own.at[2], roots.at[way, rows(z)], (1, 2)) for way, part in each]
    r_own = [own_to(10, way, part, own.at[2], roots) for way, part in each]
    r_on = [pass_on(12, way, part, roots, ((2, 1), (3, 0))) for way, part in each]
    back = [
        [tile_back(step, way) for step in (1, 2, 3) for way in both],
        [half_back(17, way, 1, part) for way, part in each],
        [half_back(19, way, 2, part) for way, part in each],
    ]

    swap_role = jnp.where(own_slot[0] == 3, 0, 1)
    swaps = jnp.logical_and(inner, jnp.logical_or(own_slot[0] == 3, own_slot[1] == 3))
    own_half = pl.ds(pl.multiple_of(jnp.where(first_half, 0, 512), 512), 512)

    def swap(number, ref):
        return pltpu.make_async_remote_copy(
            src_ref=ref, dst_ref=ref, send_sem=swap_sem.at[0, number], recv_sem=swap_sem.at[1, number],
            device_id={"tensor": 3 - t}, device_id_type=MESH,
        )

    swap_grad = [swap(step - 1, blocks.at[swap_role, rows(along(step)), own_half]) for step in (1, 2, 3)]
    swap_left = swap(3, other_left.at[swap_role, :, own_half])

    def guarded(condition, action):
        if condition is None:
            action()
        else:
            pl.when(condition)(action)

    def start(copies):
        for copy, sends, _ in copies:
            guarded(sends, copy.start)

    def arrive(copies):
        for copy, _, receives in copies:
            guarded(receives, copy.wait_recv)

    def start_where(whole):
        for copies, slots in ((b_feed, feed_slot), (b_own, own_slot)):
            for (copy, sends, _), (way, _) in zip(copies, each):
                pl.when(jnp.logical_and(sends, (slots[way] < 3) == whole))(copy.start)

    start(detour_out)
    loaded_whole(0)
    start_where(True)
    loaded_pieces(0)
    start_where(False)
    loaded_whole(1)
    loaded_pieces(1)
    start(l_feed)
    arrive(detour_out)
    start(detour_over)
    loaded_whole(2)
    loaded_pieces(2)
    start(r_feed)
    loaded_half(0)
    loaded_half(1)
    for role in both:
        blocks[role, rows(z), :] = own[0, own_slot[role]]
        roots[role, rows(z), :] = own[2, own_slot[role]]
    arrive(b_feed)
    start(b_on)
    start(r_own)
    arrive(b_own)

    @pl.when(swaps)
    def _():
        swap_grad[0].start()
        swap_grad[2].start()

    arrive(l_feed)
    pl.when(swaps)(swap_left.start)
    arrive(b_on)
    pl.when(swaps)(swap_grad[1].start)
    arrive(detour_over)
    start(detour_in)
    arrive(r_feed)
    start(r_on)

    @pl.when(swaps)
    def _():
        for copy in swap_grad + [swap_left]:
            copy.wait()

    def compute_stats(role, mine):
        quarter = z if mine else behind[role]
        slot = own_slot[role]
        flipped[...] = blocks[role, :, cols(quarter * Q, Q)].T

        def tile(n, carry):
            window = cols(n * Q, Q)
            left = matmul_nt(blocks[role, rows(quarter), :], blocks[role, rows(n), :])
            left = (left * (1.0 / BLK)).astype(jnp.bfloat16)
            right = matmul(flipped[...], blocks[role, :, window])
            right = (right * (1.0 / BLK)).astype(jnp.bfloat16)
            if mine:
                home[0, slot, :, window] = left
                home[1, slot, :, window] = right
            else:
                away[0, role, :, window] = left
                away[1, role, :, window] = right
            return carry

        lax.fori_loop(0, 4, tile, 0)

    def compute_diagonal():
        for way in both:
            feed = own[0, feed_slot[way]]
            tile = (matmul_nt(feed, feed) * (1.0 / BLK)).astype(jnp.bfloat16)
            home[0, feed_slot[way], :, cols(z * Q, Q)] = tile

    def compute_applied(role, mine):
        def tile(n, carry):
            window = cols(n * Q, Q)
            left_rows = own[1, own_slot[role]] if mine else other_left[role]
            applied[role, 1 if mine else 0, :, window] = matmul(left_rows, blocks[role, :, window]).astype(jnp.bfloat16)
            return carry

        lax.fori_loop(0, 4, tile, 0)

    compute_stats(0, False)
    compute_stats(1, False)
    start(back[0])
    for mine in (False, True):
        for role in both:
            compute_applied(role, mine)
    compute_diagonal()
    compute_stats(0, True)
    compute_stats(1, True)
    arrive(r_own)

    sums[0] = jnp.zeros((8, 128), jnp.float32)

    def compute_update(role, mine, part):
        slot = own_slot[role]

        def tile(n, carry):
            @pl.when(wanted(slot, n < 2))
            def _():
                window = cols(n * Q, Q)
                value = matmul(applied[role, 1 if mine else 0], roots[role, :, window])
                if mine:
                    home[2, slot, :, window] = value.astype(jnp.bfloat16)
                else:
                    away[2, role, :, window] = value.astype(jnp.bfloat16)
                squares = jnp.sum((value * value).reshape(Q // 8, 8, Q), axis=0)
                sums[0] += squares[:, :128] + squares[:, 128:]

            return carry

        lax.fori_loop(2 * part, 2 * part + 2, tile, 0)

    for part in halves:
        arrive(r_on[2 * part : 2 * part + 2])
        if part == 0:
            arrive(detour_in)
        for mine in (False, True):
            for role in both:
                compute_update(role, mine, part)

    def store(kind, slot):
        return pltpu.make_async_copy(
            home.at[kind, slot], outputs[kind].at[0, :, cols(Q * t + BLK * slot, BLK)], store_sem.at[kind, slot]
        )

    def outer_store(kind):
        return pltpu.make_async_copy(
            home.at[kind, 3, :, cols(jnp.where(first_half, 0, 256), 768)],
            outputs[kind].at[0, :, cols(jnp.where(first_half, 3072, 0), 768)],
            store_sem.at[kind, 3],
        )

    def inner_store(kind):
        return pltpu.make_async_copy(
            home.at[kind, 3, :, cols(jnp.where(first_half, 0, 512), 512)],
            outputs[kind].at[0, :, cols(jnp.where(first_half, 3328, 0), 512)],
            store_sem.at[kind, 3],
        )

    def edge_store(kind):
        return pltpu.make_async_copy(
            edge.at[kind], outputs[kind].at[0, :, cols(jnp.where(first_half, 0, 3584), 256)], store_sem.at[kind, 4]
        )

    def edge_over(kind):
        return pltpu.make_async_remote_copy(
            src_ref=home.at[kind, 3, :, cols(jnp.where(first_half, 768, 0), 256)], dst_ref=edge.at[kind],
            send_sem=edge_sem.at[0, kind], recv_sem=edge_sem.at[1, kind],
            device_id={"tensor": jnp.where(first_half, 1, 2)}, device_id_type=MESH,
        )

    def edge_arrives(kind):
        return pltpu.make_async_remote_copy(
            src_ref=edge.at[kind], dst_ref=edge.at[kind],
            send_sem=edge_sem.at[0, kind], recv_sem=edge_sem.at[1, kind],
            device_id={"tensor": jnp.where(first_half, 0, 3)}, device_id_type=MESH,
        )

    def deliver(kind):
        if kind < 2:
            arrive(back[kind])
            pl.when(outer)(edge_over(kind).start)
        else:
            @pl.when(t == 0)
            def _():
                arrive(back[2][2:])
                edge_over(2).start()
                arrive(back[2][:2])

            @pl.when(t > 0)
            def _():
                arrive(back[2][:2])
                pl.when(outer)(edge_over(2).start)
                arrive(back[2][2:])

        @pl.when(outer)
        def _():
            outer_store(kind).start()

        @pl.when(inner)
        def _():
            inner_store(kind).start()

        for slot in range(3):
            store(kind, slot).start()

    def share(stage, number, device):
        return pltpu.make_async_remote_copy(
            src_ref=sums.at[stage], dst_ref=landed.at[number],
            send_sem=sum_sem.at[0, number], recv_sem=sum_sem.at[1, number],
            device_id=device, device_id_type=MESH,
        )

    stages = [
        [(i - 1, z_device(i)) for i in (1, 2, 3)],
        [(i + 2, t_device(i)) for i in (1, 2, 3)],
        [(6, g_device(1))],
        [(7, g_device(2))],
        [(8, g_device(4))],
    ]
    for stage, group in enumerate(stages):
        copies = [share(stage, number, device) for number, device in group]
        for copy in copies:
            copy.start()
        if stage == 0:
            start(back[1])
            pl.when(t == 0)(lambda: start(back[2][2:] + back[2][:2]))
            pl.when(t > 0)(lambda: start(back[2]))
        if stage == len(stages) - 1:
            deliver(1)
            deliver(2)
        total = sums[stage]
        for copy in copies:
            copy.wait()
        for number, _ in group:
            total = total + landed[number]
        sums[stage + 1] = total
        if stage == 0:
            deliver(0)
    square_sum = jnp.sum(sums[len(stages)])
    scale_out[...] = 1.0 / jnp.sqrt(jnp.full((8, 128), square_sum) * (1.0 / (D * FF)) + 1e-06)

    for kind in (0, 1, 2):
        @pl.when(inner)
        def _():
            edge_arrives(kind).wait_recv()
            edge_store(kind).start()

    for kind in (0, 1, 2):
        for slot in range(3):
            store(kind, slot).wait()

        @pl.when(inner)
        def _():
            inner_store(kind).wait()
            edge_store(kind).wait()

        @pl.when(jnp.logical_not(inner))
        def _():
            outer_store(kind).wait()
            edge_over(kind).wait_send()

    for copies in [b_feed, b_own, b_on, l_feed, r_feed, r_own, r_on, detour_out, detour_over, detour_in] + back:
        for copy, sends, _ in copies:
            guarded(sends, copy.wait_send)


def shards(grad, left_roots, right_roots):
    half = jnp.bfloat16
    out = jax.ShapeDtypeStruct((1, Q, COLS), half)
    hbm = pl.BlockSpec(memory_space=pl.ANY)
    dma = pltpu.SemaphoreType.DMA
    left, right, update, scale = pl.pallas_call(
        kernel,
        out_shape=[out, out, out, jax.ShapeDtypeStruct((8, 128), jnp.float32)],
        in_specs=[pl.BlockSpec(memory_space=pltpu.HBM)] * 3,
        out_specs=[hbm] * 3 + [pl.BlockSpec(memory_space=pltpu.VMEM)],
        scratch_shapes=[
            pltpu.VMEM((3, 4, Q, BLK), half),
            pltpu.VMEM((2, BLK, BLK), half),
            pltpu.VMEM((2, BLK, BLK), half),
            pltpu.VMEM((2, Q, BLK), half),
            pltpu.VMEM((Q, BLK), half),
            pltpu.VMEM((2, 2, Q, BLK), half),
            pltpu.VMEM((3, 2, Q, BLK), half),
            pltpu.VMEM((3, 4, Q, BLK), half),
            pltpu.VMEM((3, Q, Q), half),
            pltpu.VMEM((Q, 512), half),
            pltpu.VMEM((6, 8, 128), jnp.float32),
            pltpu.VMEM((9, 8, 128), jnp.float32),
            dma((3, 3)), dma((3,)), dma((4, 3)), dma((2, 4)), dma((24, 2)), dma((24, 2)), dma((2, 9)), dma((3, 5)), dma((2, 3)),
        ],
        compiler_params=pltpu.CompilerParams(
            collective_id=0, has_side_effects=True, vmem_limit_bytes=30 * 1024 * 1024
        ),
        cost_estimate=pl.CostEstimate(flops=8_600_000_000, bytes_accessed=12_000_000, transcendentals=0),
    )(*[pltpu.with_memory_space_constraint(a, pltpu.HBM) for a in (grad, left_roots, right_roots)])
    return finish(left, right, update, scale)


def finish_kernel(left, right, update, scale, left_out, right_out, update_out, wide, narrow, sem):
    part = 64
    copies = []
    slot = 0
    for start in range(0, Q, part):
        rows = pl.ds(start, part)
        for source, target in ((left, left_out), (right, right_out)):
            wide[slot] = source[0, rows, :].astype(jnp.float32)
            copies.append(pltpu.make_async_copy(wide.at[slot], target.at[0, rows, :], sem.at[len(copies)]))
            copies[-1].start()
            slot += 1
        narrow[rows, :] = (update[0, rows, :].astype(jnp.float32) * scale[0:1, 0:1]).astype(jnp.bfloat16)
        copies.append(pltpu.make_async_copy(narrow.at[rows, :], update_out.at[0, rows, :], sem.at[len(copies)]))
        copies[-1].start()
    for copy in copies:
        copy.wait()


def finish(left, right, update, scale):
    shape = (1, Q, COLS)
    return tuple(pl.pallas_call(
        finish_kernel,
        out_shape=[jax.ShapeDtypeStruct(shape, d) for d in (jnp.float32, jnp.float32, jnp.bfloat16)],
        in_specs=[pl.BlockSpec(memory_space=pltpu.VMEM)] * 4,
        out_specs=[pl.BlockSpec(memory_space=pl.ANY)] * 3,
        scratch_shapes=[
            pltpu.VMEM((8, 64, COLS), jnp.float32), pltpu.VMEM((Q, COLS), jnp.bfloat16), pltpu.SemaphoreType.DMA((12,))
        ],
        compiler_params=pltpu.CompilerParams(vmem_limit_bytes=16 * 1024 * 1024),
    )(left, right, update, scale))


def solution(mesh):
    spec = P(None, "fsdp", "tensor")
    return jax.shard_map(shards, mesh=mesh, in_specs=(spec,) * 3, out_specs=(spec,) * 3, check_vma=False)
```

```python
import functools

import jax
import jax.numpy as jnp
from jax import lax
from jax.experimental import pallas as pl
from jax.experimental.pallas import tpu as pltpu
from jax.sharding import PartitionSpec as P

D = 8192
FF = 15360
BLK = 1024
Q = 256
RING = 4
COLS = 3840
TURN = 0
MESH = pl.DeviceIdType.MESH


def matmul(a, b):
    return lax.dot_general(a, b, (((1,), (0,)), ((), ())), preferred_element_type=jnp.float32)


def matmul_nt(a, b):
    return lax.dot_general(a, b, (((1,), (1,)), ((), ())), preferred_element_type=jnp.float32)


def kernel(
    grad, left_roots, right_roots, left_out, right_out, update_out, scale_out,
    own, blocks, roots, other_left, flipped, applied, away, home, edge, transit, sums, landed,
    load_sem, piece_sem, halo_sem, swap_sem, send_sem, recv_sem, sum_sem, store_sem, edge_sem,
):
    inputs = (grad, left_roots, right_roots)
    outputs = (left_out, right_out, update_out)
    t = lax.axis_index("tensor")
    f = lax.axis_index("fsdp")
    z = lax.rem(f, RING)
    g = lax.div(f, RING)
    inner = jnp.logical_or(t == 1, t == 2)
    outer = jnp.logical_not(inner)
    detours = lax.rem(t, 2) == 0
    first_half = t < 2

    def along(step):
        return lax.rem(z + step + RING, RING)

    def z_device(step):
        return {"fsdp": g * RING + along(step)}

    def t_device(step):
        return {"tensor": lax.rem(t + step, 4)}

    def g_device(bit):
        other = g + bit - 2 * bit * lax.rem(lax.div(g, bit), 2)
        return {"fsdp": other * RING + z}

    def rows(quarter):
        return pl.ds(pl.multiple_of(quarter * Q, Q), Q)

    def cols(start, size):
        return pl.ds(pl.multiple_of(start, Q), size)

    loads = []
    for kind in (0, 1, 2):
        for slot in range(3):
            loads.append(pltpu.make_async_copy(
                inputs[kind].at[0, :, cols(Q * t + BLK * slot, BLK)], own.at[kind, slot], load_sem.at[kind, slot]
            ))
    for copy in loads:
        copy.start()

    barrier = pltpu.get_barrier_semaphore()
    partners = [z_device(i) for i in (1, 2, 3)] + [t_device(i) for i in (1, 2, 3)] + [g_device(b) for b in (1, 2, 4)]
    for device in partners:
        pl.semaphore_signal(barrier, inc=1, device_id=device, device_id_type=MESH)
    pl.semaphore_wait(barrier, len(partners))

    def outer_piece(kind):
        return pltpu.make_async_copy(
            inputs[kind].at[0, :, cols(jnp.where(first_half, 3072, 0), 768)],
            own.at[kind, 3, :, cols(jnp.where(first_half, 0, 256), 768)],
            piece_sem.at[kind],
        )

    def inner_piece(kind):
        return pltpu.make_async_copy(
            inputs[kind].at[0, :, cols(jnp.where(first_half, 3328, 0), 512)],
            own.at[kind, 3, :, cols(jnp.where(first_half, 0, 512), 512)],
            piece_sem.at[kind],
        )

    def half_over(kind):
        return pltpu.make_async_remote_copy(
            src_ref=inputs[kind].at[0, :, cols(jnp.where(first_half, 3328, 0), 512)],
            dst_ref=own.at[kind, 3, :, cols(jnp.where(first_half, 0, 512), 512)],
            send_sem=halo_sem.at[0, kind], recv_sem=halo_sem.at[1, kind],
            device_id={"tensor": 3 - t}, device_id_type=MESH,
        )

    def quarter_over(kind):
        return pltpu.make_async_remote_copy(
            src_ref=inputs[kind].at[0, :, cols(jnp.where(first_half, 0, 3584), 256)],
            dst_ref=own.at[kind, 3, :, cols(jnp.where(first_half, 768, 0), 256)],
            send_sem=halo_sem.at[2, kind], recv_sem=halo_sem.at[3, kind],
            device_id={"tensor": jnp.where(first_half, 0, 3)}, device_id_type=MESH,
        )

    def quarter_arrives(kind):
        return pltpu.make_async_remote_copy(
            src_ref=own.at[kind, 3, :, cols(jnp.where(first_half, 768, 0), 256)],
            dst_ref=own.at[kind, 3, :, cols(jnp.where(first_half, 768, 0), 256)],
            send_sem=halo_sem.at[2, kind], recv_sem=halo_sem.at[3, kind],
            device_id={"tensor": jnp.where(first_half, 1, 2)}, device_id_type=MESH,
        )

    @pl.when(inner)
    def _():
        for kind in (0, 1, 2):
            if kind < 2:
                half_over(kind).start()
            quarter_over(kind).start()
            inner_piece(kind).start()

    @pl.when(jnp.logical_not(inner))
    def _():
        for kind in (0, 1, 2):
            outer_piece(kind).start()

    def loaded_whole(kind):
        for slot in range(3):
            loads[3 * kind + slot].wait()

    def loaded_pieces(kind):
        @pl.when(inner)
        def _():
            inner_piece(kind).wait()
            quarter_over(kind).wait_send()

        @pl.when(outer)
        def _():
            outer_piece(kind).wait()
            quarter_arrives(kind).wait_recv()

    def loaded_half(kind):
        pl.when(inner)(half_over(kind).wait)

    def send(number, way, source, target):
        return pltpu.make_async_remote_copy(
            src_ref=source, dst_ref=target,
            send_sem=send_sem.at[number, way], recv_sem=recv_sem.at[number, way],
            device_id=z_device(1 if way == 0 else 3), device_id_type=MESH,
        )

    own_slot = (along(-TURN), along(-TURN - 1))
    feed_slot = (along(1 - TURN), along(2 - TURN))
    behind = (along(-1), along(1))

    both = (0, 1)
    halves = (0, 1)

    def wanted(slot, in_first):
        return jnp.logical_or(jnp.logical_or(slot < 3, outer), in_first == first_half)

    def half_wanted(slot, part):
        return jnp.logical_or(
            jnp.logical_or(slot < 3, outer), first_half if part == 0 else jnp.logical_not(first_half)
        )

    def unless(condition, part, device):
        if part == 1 or device is None:
            return condition
        return jnp.logical_and(condition, jnp.logical_not(jnp.logical_and(detours, z == (device + TURN) % RING)))

    def columns(part):
        return pl.ds(512 * part, 512)

    def feed_to(number, way, part, source, target, skipped=(None, None)):
        copy = send(number + part, way, source.at[feed_slot[way], :, columns(part)], target.at[:, columns(part)])
        return (
            copy,
            unless(half_wanted(feed_slot[way], part), part, skipped[way]),
            unless(half_wanted(own_slot[way], part), part, skipped[1 - way]),
        )

    def own_to(number, way, part, source, full):
        copy = send(
            number + part, way, source.at[own_slot[way], :, columns(part)],
            full.at[1 - way, rows(z), columns(part)],
        )
        return copy, half_wanted(own_slot[way], part), half_wanted(own_slot[1 - way], part)

    def pass_on(number, way, part, full, skipped=((None, None), (None, None))):
        quarter = rows(behind[way])
        copy = send(
            number + part, way, full.at[way, quarter, columns(part)], full.at[1 - way, quarter, columns(part)]
        )
        return (
            copy,
            unless(half_wanted(own_slot[way], part), part, skipped[0][way]),
            unless(half_wanted(own_slot[1 - way], part), part, skipped[1][way]),
        )

    back_slot = (own_slot[1], own_slot[0])

    def tile_back(step, way):
        quarter = lax.rem(behind[1 - way] + step, RING)
        window = cols(quarter * Q, Q)
        copy = send(13 + step, way, away.at[0, 1 - way, :, window], home.at[0, back_slot[way], :, window])
        return (
            copy,
            wanted(back_slot[way], quarter < 2),
            wanted(feed_slot[1 - way], lax.rem(z + step, RING) < 2),
        )

    def half_back(number, way, kind, part):
        copy = send(
            number + part, way, away.at[kind, 1 - way, :, columns(part)],
            home.at[kind, back_slot[way], :, columns(part)],
        )
        return copy, half_wanted(back_slot[way], part), half_wanted(feed_slot[1 - way], part)

    def detour(number, way, source, target, sender):
        sender = (sender + TURN) % RING
        receiver = (sender + 1 if way == 0 else sender + 3) % RING
        return (
            send(number, way, source, target),
            jnp.logical_and(detours, z == sender),
            jnp.logical_and(detours, z == receiver),
        )

    first = columns(0)
    low = pl.ds((1 + TURN) % RING * Q, Q)
    high = pl.ds((2 + TURN) % RING * Q, Q)
    detour_out = [
        detour(21, 0, right_roots.at[0, :, cols(Q * t, 512)], transit, 2),
        detour(21, 1, right_roots.at[0, :, cols(Q * t + 2 * BLK, 512)], transit, 1),
    ]
    detour_over = [
        detour(22, 0, transit, roots.at[0, high, first], 3),
        detour(22, 1, transit, roots.at[1, low, first], 0),
    ]
    detour_in = [
        detour(23, 0, roots.at[0, high, first], roots.at[1, high, first], 0),
        detour(23, 1, roots.at[1, low, first], roots.at[0, low, first], 3),
    ]

    each = [(way, part) for part in halves for way in both]
    b_feed = [feed_to(0, way, part, own.at[0], blocks.at[way, rows(z)]) for way, part in each]
    b_own = [own_to(2, way, part, own.at[0], blocks) for way, part in each]
    b_on = [pass_on(4, way, part, blocks) for way, part in each]
    l_feed = [feed_to(6, way, part, own.at[1], other_left.at[way]) for way, part in each]
    r_feed = [feed_to(8, way, part, own.at[2], roots.at[way, rows(z)], (1, 2)) for way, part in each]
    r_own = [own_to(10, way, part, own.at[2], roots) for way, part in each]
    r_on = [pass_on(12, way, part, roots, ((2, 1), (3, 0))) for way, part in each]
    back = [
        [tile_back(step, way) for step in (1, 2, 3) for way in both],
        [half_back(17, way, 1, part) for way, part in each],
        [half_back(19, way, 2, part) for way, part in each],
    ]

    swap_role = jnp.where(own_slot[0] == 3, 0, 1)
    swaps = jnp.logical_and(inner, jnp.logical_or(own_slot[0] == 3, own_slot[1] == 3))
    own_half = pl.ds(pl.multiple_of(jnp.where(first_half, 0, 512), 512), 512)

    def swap(number, ref):
        return pltpu.make_async_remote_copy(
            src_ref=ref, dst_ref=ref, send_sem=swap_sem.at[0, number], recv_sem=swap_sem.at[1, number],
            device_id={"tensor": 3 - t}, device_id_type=MESH,
        )

    swap_grad = [swap(step - 1, blocks.at[swap_role, rows(along(step)), own_half]) for step in (1, 2, 3)]
    swap_left = swap(3, other_left.at[swap_role, :, own_half])

    def guarded(condition, action):
        if condition is None:
            action()
        else:
            pl.when(condition)(action)

    def start(copies):
        for copy, sends, _ in copies:
            guarded(sends, copy.start)

    def arrive(copies):
        for copy, _, receives in copies:
            guarded(receives, copy.wait_recv)

    def start_where(whole):
        for copies, slots in ((b_feed, feed_slot), (b_own, own_slot)):
            for (copy, sends, _), (way, _) in zip(copies, each):
                pl.when(jnp.logical_and(sends, (slots[way] < 3) == whole))(copy.start)

    start(detour_out)
    loaded_whole(0)
    start_where(True)
    loaded_pieces(0)
    start_where(False)
    loaded_whole(1)
    loaded_pieces(1)
    start(l_feed)
    arrive(detour_out)
    start(detour_over)
    loaded_whole(2)
    loaded_pieces(2)
    start(r_feed)
    loaded_half(0)
    loaded_half(1)
    for role in both:
        blocks[role, rows(z), :] = own[0, own_slot[role]]
        roots[role, rows(z), :] = own[2, own_slot[role]]
    arrive(b_feed)
    start(b_on)
    start(r_own)
    arrive(b_own)

    @pl.when(swaps)
    def _():
        swap_grad[0].start()
        swap_grad[2].start()

    arrive(l_feed)
    pl.when(swaps)(swap_left.start)
    arrive(b_on)
    pl.when(swaps)(swap_grad[1].start)
    arrive(detour_over)
    start(detour_in)
    arrive(r_feed)
    start(r_on)

    @pl.when(swaps)
    def _():
        for copy in swap_grad + [swap_left]:
            copy.wait()

    def compute_stats(role, mine):
        quarter = z if mine else behind[role]
        slot = own_slot[role]
        flipped[...] = blocks[role, :, cols(quarter * Q, Q)].T

        def tile(n, carry):
            window = cols(n * Q, Q)
            left = matmul_nt(blocks[role, rows(quarter), :], blocks[role, rows(n), :])
            left = (left * (1.0 / BLK)).astype(jnp.bfloat16)
            right = matmul(flipped[...], blocks[role, :, window])
            right = (right * (1.0 / BLK)).astype(jnp.bfloat16)
            if mine:
                home[0, slot, :, window] = left
                home[1, slot, :, window] = right
            else:
                away[0, role, :, window] = left
                away[1, role, :, window] = right
            return carry

        lax.fori_loop(0, 4, tile, 0)

    def compute_diagonal():
        for way in both:
            feed = own[0, feed_slot[way]]
            tile = (matmul_nt(feed, feed) * (1.0 / BLK)).astype(jnp.bfloat16)
            home[0, feed_slot[way], :, cols(z * Q, Q)] = tile

    def compute_applied(role, mine):
        def tile(n, carry):
            window = cols(n * Q, Q)
            left_rows = own[1, own_slot[role]] if mine else other_left[role]
            applied[role, 1 if mine else 0, :, window] = matmul(left_rows, blocks[role, :, window]).astype(jnp.bfloat16)
            return carry

        lax.fori_loop(0, 4, tile, 0)

    compute_stats(0, False)
    compute_stats(1, False)
    start(back[0])
    for mine in (False, True):
        for role in both:
            compute_applied(role, mine)
    arrive(r_own)

    sums[0] = jnp.zeros((8, 128), jnp.float32)

    def compute_update(role, mine, part):
        slot = own_slot[role]

        def tile(n, carry):
            @pl.when(wanted(slot, n < 2))
            def _():
                window = cols(n * Q, Q)
                value = matmul(applied[role, 1 if mine else 0], roots[role, :, window])
                if mine:
                    home[2, slot, :, window] = value.astype(jnp.bfloat16)
                else:
                    away[2, role, :, window] = value.astype(jnp.bfloat16)
                squares = jnp.sum((value * value).reshape(Q // 8, 8, Q), axis=0)
                sums[0] += squares[:, :128] + squares[:, 128:]

            return carry

        lax.fori_loop(2 * part, 2 * part + 2, tile, 0)

    for part in halves:
        arrive(r_on[2 * part : 2 * part + 2])
        if part == 0:
            arrive(detour_in)
        for mine in (False, True):
            for role in both:
                compute_update(role, mine, part)

    def store(kind, slot):
        return pltpu.make_async_copy(
            home.at[kind, slot], outputs[kind].at[0, :, cols(Q * t + BLK * slot, BLK)], store_sem.at[kind, slot]
        )

    def outer_store(kind):
        return pltpu.make_async_copy(
            home.at[kind, 3, :, cols(jnp.where(first_half, 0, 256), 768)],
            outputs[kind].at[0, :, cols(jnp.where(first_half, 3072, 0), 768)],
            store_sem.at[kind, 3],
        )

    def inner_store(kind):
        return pltpu.make_async_copy(
            home.at[kind, 3, :, cols(jnp.where(first_half, 0, 512), 512)],
            outputs[kind].at[0, :, cols(jnp.where(first_half, 3328, 0), 512)],
            store_sem.at[kind, 3],
        )

    def edge_store(kind):
        return pltpu.make_async_copy(
            edge.at[kind], outputs[kind].at[0, :, cols(jnp.where(first_half, 0, 3584), 256)], store_sem.at[kind, 4]
        )

    def edge_over(kind):
        return pltpu.make_async_remote_copy(
            src_ref=home.at[kind, 3, :, cols(jnp.where(first_half, 768, 0), 256)], dst_ref=edge.at[kind],
            send_sem=edge_sem.at[0, kind], recv_sem=edge_sem.at[1, kind],
            device_id={"tensor": jnp.where(first_half, 1, 2)}, device_id_type=MESH,
        )

    def edge_arrives(kind):
        return pltpu.make_async_remote_copy(
            src_ref=edge.at[kind], dst_ref=edge.at[kind],
            send_sem=edge_sem.at[0, kind], recv_sem=edge_sem.at[1, kind],
            device_id={"tensor": jnp.where(first_half, 0, 3)}, device_id_type=MESH,
        )

    def deliver(kind):
        if kind < 2:
            arrive(back[kind])
            pl.when(outer)(edge_over(kind).start)
        else:
            @pl.when(t == 0)
            def _():
                arrive(back[2][2:])
                edge_over(2).start()
                arrive(back[2][:2])

            @pl.when(t > 0)
            def _():
                arrive(back[2][:2])
                pl.when(outer)(edge_over(2).start)
                arrive(back[2][2:])

        @pl.when(outer)
        def _():
            outer_store(kind).start()

        @pl.when(inner)
        def _():
            inner_store(kind).start()

        for slot in range(3):
            store(kind, slot).start()

    def share(stage, number, device):
        return pltpu.make_async_remote_copy(
            src_ref=sums.at[stage], dst_ref=landed.at[number],
            send_sem=sum_sem.at[0, number], recv_sem=sum_sem.at[1, number],
            device_id=device, device_id_type=MESH,
        )

    stages = [
        [(i - 1, z_device(i)) for i in (1, 2, 3)],
        [(i + 2, t_device(i)) for i in (1, 2, 3)],
        [(6, g_device(1))],
        [(7, g_device(2))],
        [(8, g_device(4))],
    ]
    for stage, group in enumerate(stages):
        copies = [share(stage, number, device) for number, device in group]
        for copy in copies:
            copy.start()
        if stage == 0:
            start(back[1])
            pl.when(t == 0)(lambda: start(back[2][2:] + back[2][:2]))
            pl.when(t > 0)(lambda: start(back[2]))
        if stage == 0:
            compute_diagonal()
            compute_stats(0, True)
            compute_stats(1, True)
        if stage == len(stages) - 1:
            deliver(1)
            deliver(2)
        total = sums[stage]
        for copy in copies:
            copy.wait()
        for number, _ in group:
            total = total + landed[number]
        sums[stage + 1] = total
        if stage == 0:
            deliver(0)
    square_sum = jnp.sum(sums[len(stages)])
    scale_out[...] = 1.0 / jnp.sqrt(jnp.full((8, 128), square_sum) * (1.0 / (D * FF)) + 1e-06)

    for kind in (0, 1, 2):
        @pl.when(inner)
        def _():
            edge_arrives(kind).wait_recv()
            edge_store(kind).start()

    for kind in (0, 1, 2):
        for slot in range(3):
            store(kind, slot).wait()

        @pl.when(inner)
        def _():
            inner_store(kind).wait()
            edge_store(kind).wait()

        @pl.when(jnp.logical_not(inner))
        def _():
            outer_store(kind).wait()
            edge_over(kind).wait_send()

    for copies in [b_feed, b_own, b_on, l_feed, r_feed, r_own, r_on, detour_out, detour_over, detour_in] + back:
        for copy, sends, _ in copies:
            guarded(sends, copy.wait_send)


def shards(grad, left_roots, right_roots):
    half = jnp.bfloat16
    out = jax.ShapeDtypeStruct((1, Q, COLS), half)
    hbm = pl.BlockSpec(memory_space=pl.ANY)
    dma = pltpu.SemaphoreType.DMA
    left, right, update, scale = pl.pallas_call(
        kernel,
        out_shape=[out, out, out, jax.ShapeDtypeStruct((8, 128), jnp.float32)],
        in_specs=[pl.BlockSpec(memory_space=pltpu.HBM)] * 3,
        out_specs=[hbm] * 3 + [pl.BlockSpec(memory_space=pltpu.VMEM)],
        scratch_shapes=[
            pltpu.VMEM((3, 4, Q, BLK), half),
            pltpu.VMEM((2, BLK, BLK), half),
            pltpu.VMEM((2, BLK, BLK), half),
            pltpu.VMEM((2, Q, BLK), half),
            pltpu.VMEM((Q, BLK), half),
            pltpu.VMEM((2, 2, Q, BLK), half),
            pltpu.VMEM((3, 2, Q, BLK), half),
            pltpu.VMEM((3, 4, Q, BLK), half),
            pltpu.VMEM((3, Q, Q), half),
            pltpu.VMEM((Q, 512), half),
            pltpu.VMEM((6, 8, 128), jnp.float32),
            pltpu.VMEM((9, 8, 128), jnp.float32),
            dma((3, 3)), dma((3,)), dma((4, 3)), dma((2, 4)), dma((24, 2)), dma((24, 2)), dma((2, 9)), dma((3, 5)), dma((2, 3)),
        ],
        compiler_params=pltpu.CompilerParams(
            collective_id=0, has_side_effects=True, vmem_limit_bytes=30 * 1024 * 1024
        ),
        cost_estimate=pl.CostEstimate(flops=8_600_000_000, bytes_accessed=12_000_000, transcendentals=0),
    )(*[pltpu.with_memory_space_constraint(a, pltpu.HBM) for a in (grad, left_roots, right_roots)])
    return finish(left, right, update, scale)


def finish_kernel(left, right, update, scale, left_out, right_out, update_out, wide, narrow, sem):
    part = 64
    copies = []
    slot = 0
    for start in range(0, Q, part):
        rows = pl.ds(start, part)
        for source, target in ((left, left_out), (right, right_out)):
            wide[slot] = source[0, rows, :].astype(jnp.float32)
            copies.append(pltpu.make_async_copy(wide.at[slot], target.at[0, rows, :], sem.at[len(copies)]))
            copies[-1].start()
            slot += 1
        narrow[rows, :] = (update[0, rows, :].astype(jnp.float32) * scale[0:1, 0:1]).astype(jnp.bfloat16)
        copies.append(pltpu.make_async_copy(narrow.at[rows, :], update_out.at[0, rows, :], sem.at[len(copies)]))
        copies[-1].start()
    for copy in copies:
        copy.wait()


def finish(left, right, update, scale):
    shape = (1, Q, COLS)
    return tuple(pl.pallas_call(
        finish_kernel,
        out_shape=[jax.ShapeDtypeStruct(shape, d) for d in (jnp.float32, jnp.float32, jnp.bfloat16)],
        in_specs=[pl.BlockSpec(memory_space=pltpu.VMEM)] * 4,
        out_specs=[pl.BlockSpec(memory_space=pl.ANY)] * 3,
        scratch_shapes=[
            pltpu.VMEM((8, 64, COLS), jnp.float32), pltpu.VMEM((Q, COLS), jnp.bfloat16), pltpu.SemaphoreType.DMA((12,))
        ],
        compiler_params=pltpu.CompilerParams(vmem_limit_bytes=16 * 1024 * 1024),
    )(left, right, update, scale))


def solution(mesh):
    spec = P(None, "fsdp", "tensor")
    return jax.shard_map(shards, mesh=mesh, in_specs=(spec,) * 3, out_specs=(spec,) * 3, check_vma=False)
```
